256 devices in a mesh: pulse: 8 (over y, z_hi), range: 32 (over z_lo, x, core).
Axes of the slice: x: 4, y: 4, z: 8 (z_hi: 2, z_lo: 4; z = z_hi * 4 + z_lo), core: 2. Of those that a mesh axis runs over, the one named last changes fastest.
Arguments:
- phase_real: float32 [8192, 16384], P('pulse', 'range'), may hold values from -6 to 6
- phase_imag: float32 [8192, 16384], P('pulse', 'range'), may hold values from -6 to 6
- interp_tiles: float32 [64, 5, 128, 128], P('pulse'), may hold values from -0.25 to 0.25
- tile_index: int32 [64, 5], P('pulse'), may hold values from -2 to 65, as said below
- tile_count: int32 [64], P('pulse'), may hold values from 3 to 5
Outputs:
- image_real: float32 [8192, 16384], P(('pulse', 'range'))
- image_imag: float32 [8192, 16384], P(('pulse', 'range'))
The draws below stay inside these ranges and needn't reach their ends.
Inputs may be any that keep to these rules, and one draw needn't show every extreme that they name: `tile_index`: for output block b, slots 0 to 2 name blocks b - 1, b and b + 1 in some order, and slots 3 and 4 name blocks b - 2 and b + 2 in some order; names outside 0 to 63 stand for zero blocks.
All inputs are finite; a program needn't handle non-finite values.
Results may differ from the reference program's by a relative error of at most 0.0001.
Values sent between devices are 32-bit elements; how exact they have to be, the bound alone decides.
No kernel may reach another device: no remote copies, remote signals or barrier semaphores. Data moves between devices by JAX's collectives and lax.ppermute only.
A program may use at most 128 MiB of HBM per device.

```python
import jax
import jax.numpy as jnp
from jax import lax

S = 16384
AZ = 1024
BLOCK = 128
SLOTS = 5
P_SIZE = 8192
NB = 64
N_PULSE = 8


def draw_tile_index(key, part):
    key = jax.random.fold_in(key, 7)
    first_key, second_key = jax.random.split(key)
    scores = jax.random.randint(first_key, (NB, 3), 0, 1 << 20) * 4 + jnp.arange(3, dtype=jnp.int32)[None, :]
    ordering = jnp.argsort(scores, axis=1)
    near_offsets = ordering.astype(jnp.int32) - 1
    coin_flip = jax.random.randint(second_key, (NB, 1), 0, 2)
    far_first = 2 - 4 * coin_flip
    far_offsets = jnp.concatenate([far_first, -far_first], axis=1)
    offsets = jnp.concatenate([near_offsets, far_offsets], axis=1)
    return (jnp.arange(NB, dtype=jnp.int32)[:, None] + offsets).astype(jnp.int32)


def touch_ends(result, own_key, least, high):
    place = [jax.random.randint(jax.random.fold_in(own_key, axis), (), 0, length) for axis, length in enumerate(result.shape)]
    widest = result.shape.index(max(result.shape))
    beside = place[:widest] + [(place[widest] + 1) % result.shape[widest]] + place[widest + 1:]
    return result.at[tuple(place)].set(least).at[tuple(beside)].set(high)


def steps_of(key, extent, cuts, low, high):
    def one(position, blocks):
        draws = jax.random.uniform(jax.random.fold_in(jax.random.fold_in(key, 6), position), (blocks,), jnp.float32, low / len(cuts), high / len(cuts))
        return jnp.repeat(jnp.exp(draws), extent[position] // blocks).reshape((-1,) + (1,) * (len(extent) - position - 1))

    gain = one(*cuts[0])
    for cut in cuts[1:]:
        gain = gain * one(*cut)
    return gain


def centred(own_key, shape, scale, bound, shards=(), kind=jnp.bfloat16):
    factor_of = steps_of(own_key, shape, shards, -0.22, 0.18) if shards else 1.0
    entries = jax.random.normal(own_key, shape, jnp.float32) * scale * factor_of
    return jnp.minimum(jnp.maximum(entries, -bound), bound).astype(kind)


def setup_inputs(seed: int = 0) -> dict:
    arg_keys = jax.random.split(jax.random.key(seed), 6)
    phase_real = centred(arg_keys[0], (P_SIZE, S), 1.0, 6.0, ((0, 8), (1, 32)), jnp.float32)
    phase_imag = centred(arg_keys[1], (P_SIZE, S), 1.0, 6.0, ((0, 8), (1, 32)), jnp.float32)
    interp_tiles = centred(arg_keys[2], (NB, SLOTS, BLOCK, BLOCK), (4 * BLOCK) ** -0.5, 0.25, ((0, 8),), jnp.float32)
    tile_index = draw_tile_index(jax.random.fold_in(arg_keys[5], 71), 0)
    tile_count = touch_ends(jax.random.randint(arg_keys[4], (NB,), 3, SLOTS + 1), jax.random.fold_in(arg_keys[4], 1), 3, SLOTS).astype(jnp.int32)
    return dict(phase_real=phase_real, phase_imag=phase_imag, interp_tiles=interp_tiles, tile_index=tile_index, tile_count=tile_count)


def reference(phase_real, phase_imag, interp_tiles, tile_index, tile_count):
    stacked = jnp.stack([phase_real, phase_imag], axis=1)
    blocks = stacked.reshape(NB, BLOCK, 2, S)
    zero_blocks = jnp.zeros((2, BLOCK, 2, S), dtype=jnp.float32)
    padded = jnp.concatenate([zero_blocks, blocks, zero_blocks], axis=0)
    offsets = tile_index - jnp.arange(NB, dtype=jnp.int32)[:, None]
    live_slots = jnp.arange(SLOTS, dtype=jnp.int32)[None, :] < tile_count[:, None]
    resampled = jnp.zeros((NB, BLOCK, 2, S), dtype=jnp.float32)
    for offset in range(-2, 3):
        selector = ((offsets == offset) & live_slots).astype(jnp.float32)
        weights = jnp.sum(interp_tiles * selector[:, :, None, None], axis=1)
        resampled = resampled + jnp.einsum("bpq,bqcs->bpcs", weights, padded[2 + offset:2 + offset + NB],
                                           precision=lax.Precision.HIGHEST)
    subapertures = resampled.reshape(N_PULSE, AZ, 2, S)
    spectrum = lax.complex(subapertures[:, :, 0, :], subapertures[:, :, 1, :])
    spectrum = jnp.fft.fft(spectrum, axis=2, norm="ortho")
    spectrum = jnp.fft.fft(spectrum, axis=1, norm="ortho")
    spectrum = spectrum.reshape(P_SIZE, S)
    return jnp.real(spectrum).astype(jnp.float32), jnp.imag(spectrum).astype(jnp.float32)
```

```python
import functools
import math

import jax
import jax.numpy as jnp
import ml_dtypes
import numpy as np
from jax import lax
from jax.experimental import pallas as pl
from jax.experimental.pallas import tpu as pltpu
from jax.sharding import PartitionSpec as P

S = 16384
AZ = 1024
BLOCK = 128
SLOTS = 5
HALO = 2 * BLOCK
LANES = 128
PARTS = (4,)
BF16 = jnp.bfloat16
F32 = jnp.float32


def unit_roots(numerators, length):
    angles = 2.0 * math.pi * (numerators % length) / length
    return np.cos(angles), -np.sin(angles)


def halves(table):
    high = table.astype(ml_dtypes.bfloat16)
    low = (table - high.astype(np.float64)).astype(ml_dtypes.bfloat16)
    return high, low


def azimuth_tables():
    idx = np.arange(256)
    real, imag = unit_roots(idx[:, None] * idx[None, :], 256)
    high, low = halves(np.concatenate([real, imag], axis=0) / 32.0)
    turns = []
    for a in range(1, 4):
        turn = np.stack(unit_roots(a * idx, 1024))
        turns.append(np.broadcast_to(turn[:, :, None], (2, 256, LANES)))
    return high, low, np.stack(turns).astype(np.float32)


def range_tables(parts):
    idx = np.arange(128)
    order = []
    first = 0
    for width in parts:
        for source in range(32):
            order += [4 * source + first + c for c in range(width)]
        first += width
    order = np.array(order)
    real, imag = unit_roots(idx[:, None] * order[None, :], 128)
    inner = np.block([[real, -imag], [imag, real]])
    turn = np.stack(unit_roots(idx[:, None] * idx[None, :], S)).astype(np.float32)
    real, imag = unit_roots(idx[:, None] * idx[None, :], 128)
    outer = np.block([[real, -imag], [imag, real]]) / 128.0
    return (*halves(inner), turn, *halves(outer))


def split(value):
    high = value.astype(BF16)
    return high, (value - high.astype(F32)).astype(BF16)


def dot(a, b, dims=(((1,), (0,)), ((), ()))):
    return lax.dot_general(a, b, dims, preferred_element_type=F32)


def azimuth_kernel(re_ref, im_ref, top_ref, bot_ref, wh_ref, wl_ref, dh_ref, dl_ref, tw_ref, out_ref, xh, xl, yh, yl):
    def put(row, real, imag):
        high, low = split(jnp.concatenate([real, imag], axis=1))
        xh[row : row + BLOCK, :] = high
        xl[row : row + BLOCK, :] = low

    for i in range(2):
        rows = slice(i * BLOCK, (i + 1) * BLOCK)
        put(i * BLOCK, top_ref[0, rows], top_ref[1, rows])
        put(HALO + AZ + i * BLOCK, bot_ref[0, rows], bot_ref[1, rows])
    for i in range(AZ // BLOCK):
        rows = slice(i * BLOCK, (i + 1) * BLOCK)
        put(HALO + i * BLOCK, re_ref[rows], im_ref[rows])
    for b in range(AZ // BLOCK):
        rows = slice(b * BLOCK, (b + SLOTS) * BLOCK)
        cells = dot(wh_ref[b], xh[rows]) + dot(wl_ref[b], xh[rows]) + dot(wh_ref[b], xl[rows])
        high, low = split(cells)
        for a in range(4):
            yh[a, b * 32 : (b + 1) * 32] = high[a * 32 : (a + 1) * 32]
            yl[a, b * 32 : (b + 1) * 32] = low[a * 32 : (a + 1) * 32]
    real, imag = [], []
    for a in range(4):
        four = dot(dh_ref[...], yh[a]) + dot(dl_ref[...], yh[a]) + dot(dh_ref[...], yl[a])
        vr = four[:256, :LANES] - four[256:, LANES:]
        vi = four[:256, LANES:] + four[256:, :LANES]
        if a:
            tr, ti = tw_ref[a - 1, 0], tw_ref[a - 1, 1]
            vr, vi = vr * tr - vi * ti, vr * ti + vi * tr
        real.append(vr)
        imag.append(vi)
    er, ei, fr, fi = real[0] + real[2], imag[0] + imag[2], real[0] - real[2], imag[0] - imag[2]
    gr, gi, hr, hi = real[1] + real[3], imag[1] + imag[3], real[1] - real[3], imag[1] - imag[3]
    bins = [(er + gr, ei + gi), (fr + hi, fi - hr), (er - gr, ei - gi), (fr - hi, fi + hr)]
    for quarter in range(4):
        for part in range(2):
            for t in range(8):
                out_ref[quarter * 8 + t, 0, part] = bins[quarter][part][t * 32 : (t + 1) * 32]


def azimuth(first, width, phase_real, phase_imag, top, bot, weights, tables):
    fixed = lambda *shape: pl.BlockSpec(shape, lambda i: (0,) * len(shape))
    return pl.pallas_call(
        azimuth_kernel,
        grid=(width,),
        in_specs=[
            pl.BlockSpec((AZ, LANES), lambda i: (0, first + i)),
            pl.BlockSpec((AZ, LANES), lambda i: (0, first + i)),
            pl.BlockSpec((2, HALO, LANES), lambda i: (0, 0, i)),
            pl.BlockSpec((2, HALO, LANES), lambda i: (0, 0, i)),
            fixed(8, BLOCK, SLOTS * BLOCK),
            fixed(8, BLOCK, SLOTS * BLOCK),
            fixed(512, 256),
            fixed(512, 256),
            fixed(3, 2, 256, LANES),
        ],
        out_specs=pl.BlockSpec((32, 1, 2, 32, LANES), lambda i: (0, i, 0, 0, 0)),
        out_shape=jax.ShapeDtypeStruct((32, width, 2, 32, LANES), F32),
        scratch_shapes=[
            pltpu.VMEM((AZ + 2 * HALO, 2 * LANES), BF16),
            pltpu.VMEM((AZ + 2 * HALO, 2 * LANES), BF16),
            pltpu.VMEM((4, 256, 2 * LANES), BF16),
            pltpu.VMEM((4, 256, 2 * LANES), BF16),
        ],
        compiler_params=pltpu.CompilerParams(vmem_limit_bytes=40 * 1024 * 1024),
        cost_estimate=pl.CostEstimate(
            flops=6 * width * 256 * (AZ * 640 + AZ * 512), bytes_accessed=width * 2 * 2**20, transcendentals=0
        ),
        name="azimuth",
    )(phase_real, phase_imag, top, bot, *weights, *tables)


def range_kernel(parts, *refs):
    cells = refs[: len(parts)]
    ah_ref, al_ref, tw_ref, bh_ref, bl_ref, re_ref, im_ref, held = refs[len(parts) :]
    flat = [ref.reshape(32 * width * 16, LANES) for ref, width in zip(cells, parts)]

    def rows_of(part, k):
        return jnp.concatenate(
            [ref[pl.ds(part * 8 + k, 32 * width, stride=16), :] for ref, width in zip(flat, parts)], axis=0
        )

    tr, ti = tw_ref[0], tw_ref[1]
    for pair in range(4):
        k0, k1 = 2 * pair, 2 * pair + 1
        full = jnp.concatenate(
            [jnp.concatenate([rows_of(part, k) for k in (k0, k1)], axis=1) for part in range(2)], axis=0
        )
        high, low = split(full)
        inner = dot(ah_ref[...], high) + dot(al_ref[...], high) + dot(ah_ref[...], low)
        turned = []
        for i in range(2):
            yr, yi = inner[:128, i * LANES : (i + 1) * LANES], inner[128:, i * LANES : (i + 1) * LANES]
            turned.append(jnp.concatenate([yr * tr - yi * ti, yr * ti + yi * tr], axis=1))
        high, low = split(jnp.concatenate(turned, axis=0))
        flip = (((1,), (1,)), ((), ()))
        outer = dot(bh_ref[...], high, flip) + dot(bl_ref[...], high, flip) + dot(bh_ref[...], low, flip)
        for i, k in enumerate((k0, k1)):
            for part in range(2):
                held[part, k * 128 : (k + 1) * 128] = outer[
                    part * 128 : (part + 1) * 128, i * LANES : (i + 1) * LANES
                ]
    for m in range(128):
        re_ref[:, m * LANES : (m + 1) * LANES] = held[0, pl.ds(m, 8, stride=128), :]
        im_ref[:, m * LANES : (m + 1) * LANES] = held[1, pl.ds(m, 8, stride=128), :]


def range_transform(parts, cells, tables):
    fixed = lambda *shape: pl.BlockSpec(shape, lambda g: (0,) * len(shape))
    return pl.pallas_call(
        functools.partial(range_kernel, parts),
        grid=(4,),
        in_specs=[pl.BlockSpec((32, width, 2, 8, LANES), lambda g: (0, 0, 0, g, 0)) for width in parts]
        + [fixed(256, 256), fixed(256, 256), fixed(2, 128, LANES), fixed(256, 256), fixed(256, 256)],
        out_specs=[pl.BlockSpec((8, S), lambda g: (g, 0))] * 2,
        out_shape=[jax.ShapeDtypeStruct((32, S), F32)] * 2,
        scratch_shapes=[pltpu.VMEM((2, 8 * 128, LANES), F32)],
        compiler_params=pltpu.CompilerParams(vmem_limit_bytes=40 * 1024 * 1024),
        cost_estimate=pl.CostEstimate(flops=4 * 32 * S * 256 * 3, bytes_accessed=8 * 2**20, transcendentals=0),
        name="range",
    )(*cells, *tables)


def resampling_weights(interp_tiles, tile_index, tile_count):
    tiles_dev = interp_tiles.shape[0]
    first_block = lax.axis_index("pulse") * tiles_dev
    offsets = tile_index - (first_block + jnp.arange(tiles_dev, dtype=jnp.int32))[:, None]
    live = jnp.arange(SLOTS, dtype=jnp.int32)[None, :] < tile_count[:, None]
    places = jnp.arange(-2, 3, dtype=jnp.int32)
    chosen = ((offsets[:, None, :] == places[None, :, None]) & live[:, None, :]).astype(F32)
    weights = jnp.sum(interp_tiles[:, None] * chosen[:, :, :, None, None], axis=2)
    weights = weights.reshape(tiles_dev, SLOTS, 32, 4, BLOCK).transpose(0, 3, 2, 1, 4)
    weights = weights.reshape(tiles_dev, BLOCK, SLOTS * BLOCK)
    high = lax.reduce_precision(weights, 8, 7)
    return high.astype(BF16), (weights - high).astype(BF16)


def shards(phase_real, phase_imag, interp_tiles, tile_index, tile_count):
    count = lax.axis_size("pulse")
    up = [(i, i + 1) for i in range(count - 1)]
    down = [(i + 1, i) for i in range(count - 1)]
    weights = resampling_weights(interp_tiles, tile_index, tile_count)
    tables = azimuth_tables()
    ends = []
    first = 0
    for width in PARTS:
        columns = slice(first * LANES, (first + width) * LANES)
        tail = jnp.stack([phase_real[AZ - HALO :, columns], phase_imag[AZ - HALO :, columns]])
        head = jnp.stack([phase_real[:HALO, columns], phase_imag[:HALO, columns]])
        ends.append((lax.ppermute(tail, "pulse", up), lax.ppermute(head, "pulse", down)))
        first += width
    cells = []
    first = 0
    for width, (top, bot) in zip(PARTS, ends):
        sent = azimuth(first, width, phase_real, phase_imag, top, bot, weights, tables)
        cells.append(lax.all_to_all(sent, "range", split_axis=0, concat_axis=0, tiled=True))
        first += width
    return tuple(range_transform(PARTS, cells, range_tables(PARTS)))


def solution(mesh):
    placed = (
        P("pulse", "range"),
        P("pulse", "range"),
        P("pulse", None, None, None),
        P("pulse", None),
        P("pulse"),
    )
    return jax.shard_map(
        shards,
        mesh=mesh,
        in_specs=placed,
        out_specs=(P(("pulse", "range"), None), P(("pulse", "range"), None)),
        check_vma=False,
    )
```

```python
import functools
import math

import jax
import jax.numpy as jnp
import ml_dtypes
import numpy as np
from jax import lax
from jax.experimental import pallas as pl
from jax.experimental.pallas import tpu as pltpu
from jax.sharding import PartitionSpec as P

S = 16384
AZ = 1024
BLOCK = 128
SLOTS = 5
HALO = 2 * BLOCK
LANES = 128
PARTS = (2, 2)
GROUPS = 4
BF16 = jnp.bfloat16
F32 = jnp.float32


def unit_roots(numerators, length):
    angles = 2.0 * math.pi * (numerators % length) / length
    return np.cos(angles), -np.sin(angles)


def halves(table):
    high = table.astype(ml_dtypes.bfloat16)
    low = (table - high.astype(np.float64)).astype(ml_dtypes.bfloat16)
    return high, low


def azimuth_tables():
    idx = np.arange(256)
    real, imag = unit_roots(idx[:, None] * idx[None, :], 256)
    high, low = halves(np.concatenate([real, imag], axis=0) / 32.0)
    turns = []
    for a in range(1, 4):
        turn = np.stack(unit_roots(a * idx, 1024))
        turns.append(np.broadcast_to(turn[:, :, None], (2, 256, LANES)))
    return high, low, np.stack(turns).astype(np.float32)


def range_tables(parts):
    idx = np.arange(128)
    order = []
    first = 0
    for width in parts:
        for source in range(32):
            order += [4 * source + first + c for c in range(width)]
        first += width
    order = np.array(order)
    real, imag = unit_roots(idx[:, None] * order[None, :], 128)
    inner = np.block([[real, -imag], [imag, real]])
    turn = np.stack(unit_roots(idx[:, None] * idx[None, :], S)).astype(np.float32)
    real, imag = unit_roots(idx[:, None] * idx[None, :], 128)
    outer = np.block([[real, -imag], [imag, real]]) / 128.0
    return (*halves(inner), turn, *halves(outer))


def split(value):
    high = value.astype(BF16)
    return high, (value - high.astype(F32)).astype(BF16)


def dot(a, b, dims=(((1,), (0,)), ((), ()))):
    return lax.dot_general(a, b, dims, preferred_element_type=F32)


def azimuth_kernel(re_ref, im_ref, top_ref, bot_ref, wh_ref, wl_ref, dh_ref, dl_ref, tw_ref, out_ref, xh, xl, yh, yl):
    def put(row, real, imag):
        high, low = split(jnp.concatenate([real, imag], axis=1))
        xh[row : row + BLOCK, :] = high
        xl[row : row + BLOCK, :] = low

    for i in range(2):
        rows = slice(i * BLOCK, (i + 1) * BLOCK)
        put(i * BLOCK, top_ref[0, rows], top_ref[1, rows])
        put(HALO + AZ + i * BLOCK, bot_ref[0, rows], bot_ref[1, rows])
    for i in range(AZ // BLOCK):
        rows = slice(i * BLOCK, (i + 1) * BLOCK)
        put(HALO + i * BLOCK, re_ref[rows], im_ref[rows])
    for b in range(AZ // BLOCK):
        rows = slice(b * BLOCK, (b + SLOTS) * BLOCK)
        cells = dot(wh_ref[b], xh[rows]) + dot(wl_ref[b], xh[rows]) + dot(wh_ref[b], xl[rows])
        high, low = split(cells)
        for a in range(4):
            yh[a, b * 32 : (b + 1) * 32] = high[a * 32 : (a + 1) * 32]
            yl[a, b * 32 : (b + 1) * 32] = low[a * 32 : (a + 1) * 32]
    real, imag = [], []
    for a in range(4):
        four = dot(dh_ref[...], yh[a]) + dot(dl_ref[...], yh[a]) + dot(dh_ref[...], yl[a])
        vr = four[:256, :LANES] - four[256:, LANES:]
        vi = four[:256, LANES:] + four[256:, :LANES]
        if a:
            tr, ti = tw_ref[a - 1, 0], tw_ref[a - 1, 1]
            vr, vi = vr * tr - vi * ti, vr * ti + vi * tr
        real.append(vr)
        imag.append(vi)
    er, ei, fr, fi = real[0] + real[2], imag[0] + imag[2], real[0] - real[2], imag[0] - imag[2]
    gr, gi, hr, hi = real[1] + real[3], imag[1] + imag[3], real[1] - real[3], imag[1] - imag[3]
    bins = [(er + gr, ei + gi), (fr + hi, fi - hr), (er - gr, ei - gi), (fr - hi, fi + hr)]
    for quarter in range(4):
        for part in range(2):
            for t in range(8):
                out_ref[quarter * 8 + t, 0, part] = bins[quarter][part][t * 32 : (t + 1) * 32]


def azimuth(first, width, phase_real, phase_imag, top, bot, weights, tables):
    fixed = lambda *shape: pl.BlockSpec(shape, lambda i: (0,) * len(shape))
    return pl.pallas_call(
        azimuth_kernel,
        grid=(width,),
        in_specs=[
            pl.BlockSpec((AZ, LANES), lambda i: (0, first + i)),
            pl.BlockSpec((AZ, LANES), lambda i: (0, first + i)),
            pl.BlockSpec((2, HALO, LANES), lambda i: (0, 0, i)),
            pl.BlockSpec((2, HALO, LANES), lambda i: (0, 0, i)),
            fixed(8, BLOCK, SLOTS * BLOCK),
            fixed(8, BLOCK, SLOTS * BLOCK),
            fixed(512, 256),
            fixed(512, 256),
            fixed(3, 2, 256, LANES),
        ],
        out_specs=pl.BlockSpec((32, 1, 2, 32, LANES), lambda i: (0, i, 0, 0, 0)),
        out_shape=jax.ShapeDtypeStruct((32, width, 2, 32, LANES), F32),
        scratch_shapes=[
            pltpu.VMEM((AZ + 2 * HALO, 2 * LANES), BF16),
            pltpu.VMEM((AZ + 2 * HALO, 2 * LANES), BF16),
            pltpu.VMEM((4, 256, 2 * LANES), BF16),
            pltpu.VMEM((4, 256, 2 * LANES), BF16),
        ],
        compiler_params=pltpu.CompilerParams(vmem_limit_bytes=40 * 1024 * 1024),
        cost_estimate=pl.CostEstimate(
            flops=6 * width * 256 * (AZ * 640 + AZ * 512) * (100 if first else 1), bytes_accessed=width * 2 * 2**20, transcendentals=0
        ),
        name="azimuth",
    )(phase_real, phase_imag, top, bot, *weights, *tables)


def range_kernel(parts, *refs):
    cells = refs[: len(parts)]
    ah_ref, al_ref, tw_ref, bh_ref, bl_ref, re_ref, im_ref, held = refs[len(parts) :]
    flat = [ref.reshape(32 * width * 16, LANES) for ref, width in zip(cells, parts)]

    def rows_of(part, k):
        return jnp.concatenate(
            [ref[pl.ds(part * 8 + k, 32 * width, stride=16), :] for ref, width in zip(flat, parts)], axis=0
        )

    tr, ti = tw_ref[0], tw_ref[1]
    for pair in range(4):
        k0, k1 = 2 * pair, 2 * pair + 1
        full = jnp.concatenate(
            [jnp.concatenate([rows_of(part, k) for k in (k0, k1)], axis=1) for part in range(2)], axis=0
        )
        high, low = split(full)
        inner = dot(ah_ref[...], high) + dot(al_ref[...], high) + dot(ah_ref[...], low)
        turned = []
        for i in range(2):
            yr, yi = inner[:128, i * LANES : (i + 1) * LANES], inner[128:, i * LANES : (i + 1) * LANES]
            turned.append(jnp.concatenate([yr * tr - yi * ti, yr * ti + yi * tr], axis=1))
        high, low = split(jnp.concatenate(turned, axis=0))
        flip = (((1,), (1,)), ((), ()))
        outer = dot(bh_ref[...], high, flip) + dot(bl_ref[...], high, flip) + dot(bh_ref[...], low, flip)
        for i, k in enumerate((k0, k1)):
            for part in range(2):
                held[part, k * 128 : (k + 1) * 128] = outer[
                    part * 128 : (part + 1) * 128, i * LANES : (i + 1) * LANES
                ]
    for m in range(128):
        re_ref[:, m * LANES : (m + 1) * LANES] = held[0, pl.ds(m, 8, stride=128), :]
        im_ref[:, m * LANES : (m + 1) * LANES] = held[1, pl.ds(m, 8, stride=128), :]


def range_transform(parts, cells, tables):
    fixed = lambda *shape: pl.BlockSpec(shape, lambda g: (0,) * len(shape))
    return pl.pallas_call(
        functools.partial(range_kernel, parts),
        grid=(4,),
        in_specs=[pl.BlockSpec((32, width, 2, 8, LANES), lambda g: (0, 0, 0, g, 0)) for width in parts]
        + [fixed(256, 256), fixed(256, 256), fixed(2, 128, LANES), fixed(256, 256), fixed(256, 256)],
        out_specs=[pl.BlockSpec((8, S), lambda g: (g, 0))] * 2,
        out_shape=[jax.ShapeDtypeStruct((32, S), F32)] * 2,
        scratch_shapes=[pltpu.VMEM((2, 8 * 128, LANES), F32)],
        compiler_params=pltpu.CompilerParams(vmem_limit_bytes=40 * 1024 * 1024),
        cost_estimate=pl.CostEstimate(flops=4 * 32 * S * 256 * 3, bytes_accessed=8 * 2**20, transcendentals=0),
        name="range",
    )(*cells, *tables)


def resampling_weights(interp_tiles, tile_index, tile_count):
    tiles_dev = interp_tiles.shape[0]
    first_block = lax.axis_index("pulse") * tiles_dev
    offsets = tile_index - (first_block + jnp.arange(tiles_dev, dtype=jnp.int32))[:, None]
    live = jnp.arange(SLOTS, dtype=jnp.int32)[None, :] < tile_count[:, None]
    places = jnp.arange(-2, 3, dtype=jnp.int32)
    chosen = ((offsets[:, None, :] == places[None, :, None]) & live[:, None, :]).astype(F32)
    weights = jnp.sum(interp_tiles[:, None] * chosen[:, :, :, None, None], axis=2)
    weights = weights.reshape(tiles_dev, SLOTS, 32, 4, BLOCK).transpose(0, 3, 2, 1, 4)
    weights = weights.reshape(tiles_dev, BLOCK, SLOTS * BLOCK)
    high = lax.reduce_precision(weights, 8, 7)
    return high.astype(BF16), (weights - high).astype(BF16)


def shards(phase_real, phase_imag, interp_tiles, tile_index, tile_count):
    count = lax.axis_size("pulse")
    up = [(i, i + 1) for i in range(count - 1)]
    down = [(i + 1, i) for i in range(count - 1)]
    weights = resampling_weights(interp_tiles, tile_index, tile_count)
    tables = azimuth_tables()
    me = lax.axis_index("pulse")
    ends = []
    first = 0
    for width in PARTS:
        columns = slice(first * LANES, (first + width) * LANES)
        tail = jnp.stack([phase_real[AZ - HALO :, columns], phase_imag[AZ - HALO :, columns]])
        head = jnp.stack([phase_real[:HALO, columns], phase_imag[:HALO, columns]])
        first += width
        if first < GROUPS:
            ends.append((lax.ppermute(tail, "pulse", up), lax.ppermute(head, "pulse", down)))
            continue
        relayed = lax.ppermute(jnp.where(me == 2, head, tail), "pulse", [(2, 0), (5, 7)])
        relayed = lax.ppermute(relayed, "pulse", [(0, 1), (7, 6)])
        top = lax.ppermute(tail, "pulse", [pair for pair in up if pair != (5, 6)])
        bot = lax.ppermute(head, "pulse", [pair for pair in down if pair != (2, 1)])
        ends.append((jnp.where(me == 6, relayed, top), jnp.where(me == 1, relayed, bot)))
    cells = []
    first = 0
    for width, (top, bot) in zip(PARTS, ends):
        sent = azimuth(first, width, phase_real, phase_imag, top, bot, weights, tables)
        cells.append(lax.all_to_all(sent, "range", split_axis=0, concat_axis=0, tiled=True))
        first += width
    return tuple(range_transform(PARTS, cells, range_tables(PARTS)))


def solution(mesh):
    placed = (
        P("pulse", "range"),
        P("pulse", "range"),
        P("pulse", None, None, None),
        P("pulse", None),
        P("pulse"),
    )
    return jax.shard_map(
        shards,
        mesh=mesh,
        in_specs=placed,
        out_specs=(P(("pulse", "range"), None), P(("pulse", "range"), None)),
        check_vma=False,
    )
```

```python
import math

import jax
import jax.numpy as jnp
import ml_dtypes
import numpy as np
from jax import lax
from jax.experimental import pallas as pl
from jax.experimental.pallas import tpu as pltpu
from jax.sharding import PartitionSpec as P

S = 16384
AZ = 1024
BLOCK = 128
SLOTS = 5
HALO = 2 * BLOCK
LANES = 128
CHUNKS = ((0, 2), (1, 3))
BF16 = jnp.bfloat16
F32 = jnp.float32


def unit_roots(numerators, length):
    angles = 2.0 * math.pi * (numerators % length) / length
    return np.cos(angles), -np.sin(angles)


def halves(table):
    high = table.astype(ml_dtypes.bfloat16)
    low = (table - high.astype(np.float64)).astype(ml_dtypes.bfloat16)
    return high, low


def azimuth_tables():
    idx = np.arange(256)
    real, imag = unit_roots(idx[:, None] * idx[None, :], 256)
    high, low = halves(np.concatenate([real, imag], axis=0) / 32.0)
    turns = []
    for a in range(1, 4):
        turn = np.stack(unit_roots(a * idx, 1024))
        turns.append(np.broadcast_to(turn[:, :, None], (2, 256, LANES)))
    return high, low, np.stack(turns).astype(np.float32)


def complex_matrix(real, imag):
    return np.block([[real, -imag], [imag, real]])


def range_tables():
    idx = np.arange(128)
    half = np.arange(64)
    even = halves(complex_matrix(*unit_roots(half[:, None] * half[None, :], 64)))
    odd = halves(complex_matrix(*unit_roots(half[:, None] * (2 * half[None, :] + 1), 128)))
    turn = np.stack(unit_roots(idx[:, None] * idx[None, :], S)).astype(np.float32)
    outer = halves(complex_matrix(*unit_roots(idx[:, None] * idx[None, :], 128)) / 128.0)
    return even, (*odd, turn, np.concatenate(outer, axis=0))


def split(value):
    high = value.astype(BF16)
    return high, (value - high.astype(F32)).astype(BF16)


def dot(a, b, dims=(((1,), (0,)), ((), ()))):
    return lax.dot_general(a, b, dims, preferred_element_type=F32)


def azimuth_kernel(re_ref, im_ref, top_ref, bot_ref, wh_ref, wl_ref, dh_ref, dl_ref, tw_ref, out_ref, xh, xl, yh, yl):
    def put(row, real, imag):
        high, low = split(jnp.concatenate([real, imag], axis=1))
        xh[row : row + BLOCK, :] = high
        xl[row : row + BLOCK, :] = low

    for i in range(2):
        rows = slice(i * BLOCK, (i + 1) * BLOCK)
        put(i * BLOCK, top_ref[0, rows], top_ref[1, rows])
        put(HALO + AZ + i * BLOCK, bot_ref[0, rows], bot_ref[1, rows])
    for i in range(AZ // BLOCK):
        rows = slice(i * BLOCK, (i + 1) * BLOCK)
        put(HALO + i * BLOCK, re_ref[rows], im_ref[rows])
    for b in range(AZ // BLOCK):
        rows = slice(b * BLOCK, (b + SLOTS) * BLOCK)
        cells = dot(wh_ref[b], xh[rows]) + dot(wl_ref[b], xh[rows]) + dot(wh_ref[b], xl[rows])
        high, low = split(cells)
        for a in range(4):
            yh[a, b * 32 : (b + 1) * 32] = high[a * 32 : (a + 1) * 32]
            yl[a, b * 32 : (b + 1) * 32] = low[a * 32 : (a + 1) * 32]
    real, imag = [], []
    for a in range(4):
        four = dot(dh_ref[...], yh[a]) + dot(dl_ref[...], yh[a]) + dot(dh_ref[...], yl[a])
        vr = four[:256, :LANES] - four[256:, LANES:]
        vi = four[:256, LANES:] + four[256:, :LANES]
        if a:
            tr, ti = tw_ref[a - 1, 0], tw_ref[a - 1, 1]
            vr, vi = vr * tr - vi * ti, vr * ti + vi * tr
        real.append(vr)
        imag.append(vi)
    er, ei, fr, fi = real[0] + real[2], imag[0] + imag[2], real[0] - real[2], imag[0] - imag[2]
    gr, gi, hr, hi = real[1] + real[3], imag[1] + imag[3], real[1] - real[3], imag[1] - imag[3]
    bins = [(er + gr, ei + gi), (fr + hi, fi - hr), (er - gr, ei - gi), (fr - hi, fi + hr)]
    for quarter in range(4):
        for part in range(2):
            for t in range(8):
                out_ref[quarter * 8 + t, 0, part] = bins[quarter][part][t * 32 : (t + 1) * 32]


def azimuth(groups, last, phase_real, phase_imag, top, bot, weights, tables):
    fixed = lambda *shape: pl.BlockSpec(shape, lambda i: (0,) * len(shape))
    return pl.pallas_call(
        azimuth_kernel,
        grid=(len(groups),),
        in_specs=[
            pl.BlockSpec((AZ, LANES), lambda i: (0, groups[0] + 2 * i)),
            pl.BlockSpec((AZ, LANES), lambda i: (0, groups[0] + 2 * i)),
            pl.BlockSpec((2, HALO, LANES), lambda i: (0, 0, i)),
            pl.BlockSpec((2, HALO, LANES), lambda i: (0, 0, i)),
            fixed(8, BLOCK, SLOTS * BLOCK),
            fixed(8, BLOCK, SLOTS * BLOCK),
            fixed(512, 256),
            fixed(512, 256),
            fixed(3, 2, 256, LANES),
        ],
        out_specs=pl.BlockSpec((32, 1, 2, 32, LANES), lambda i: (0, i, 0, 0, 0)),
        out_shape=jax.ShapeDtypeStruct((32, len(groups), 2, 32, LANES), F32),
        scratch_shapes=[
            pltpu.VMEM((AZ + 2 * HALO, 2 * LANES), BF16),
            pltpu.VMEM((AZ + 2 * HALO, 2 * LANES), BF16),
            pltpu.VMEM((4, 256, 2 * LANES), BF16),
            pltpu.VMEM((4, 256, 2 * LANES), BF16),
        ],
        compiler_params=pltpu.CompilerParams(vmem_limit_bytes=40 * 1024 * 1024),
        cost_estimate=pl.CostEstimate(
            flops=6 * 512 * (AZ * 640 + AZ * 512) * (100 if last else 1), bytes_accessed=4 * 2**20, transcendentals=0
        ),
        name="azimuth",
    )(phase_real, phase_imag, top, bot, *weights, *tables)


def block_dft(cells_ref, high_ref, low_ref, pair):
    flat = cells_ref.reshape(64 * 16, LANES)
    full = jnp.concatenate(
        [
            jnp.concatenate([flat[pl.ds(part * 8 + 2 * pair + i, 64, stride=16), :] for i in range(2)], axis=1)
            for part in range(2)
        ],
        axis=0,
    )
    high, low = split(full)
    wide = jnp.concatenate([high_ref[...], low_ref[...], high_ref[...]], axis=1)
    return dot(wide, jnp.concatenate([high, high, low], axis=0))


def even_kernel(cells_ref, high_ref, low_ref, out_ref):
    for pair in range(4):
        both = block_dft(cells_ref, high_ref, low_ref, pair)
        for i in range(2):
            out_ref[2 * pair + i] = both[:, i * LANES : (i + 1) * LANES]


def even_blocks(cells, tables):
    return pl.pallas_call(
        even_kernel,
        grid=(4,),
        in_specs=[
            pl.BlockSpec((32, 2, 2, 8, LANES), lambda g: (0, 0, 0, g, 0)),
            pl.BlockSpec((128, 128), lambda g: (0, 0)),
            pl.BlockSpec((128, 128), lambda g: (0, 0)),
        ],
        out_specs=pl.BlockSpec((8, 128, LANES), lambda g: (g, 0, 0)),
        out_shape=jax.ShapeDtypeStruct((32, 128, LANES), F32),
        compiler_params=pltpu.CompilerParams(vmem_limit_bytes=40 * 1024 * 1024),
        cost_estimate=pl.CostEstimate(flops=32 * S * 128 * 6, bytes_accessed=4 * 2**20, transcendentals=0),
        name="even",
    )(cells, *tables)


def range_kernel(cells_ref, even_ref, ah_ref, al_ref, tw_ref, b_ref, re_ref, im_ref):
    images = [ref.reshape(128 * 8, LANES) for ref in (re_ref, im_ref)]
    for pair in range(4):
        odd = block_dft(cells_ref, ah_ref, al_ref, pair)
        turned = []
        for i in range(2):
            k = 2 * pair + i
            lanes = slice(i * LANES, (i + 1) * LANES)
            er, ei, fr, fi = even_ref[k, :64], even_ref[k, 64:], odd[:64, lanes], odd[64:, lanes]
            for yr, yi, rows in ((er + fr, ei + fi, slice(0, 64)), (er - fr, ei - fi, slice(64, 128))):
                tr, ti = tw_ref[0, rows], tw_ref[1, rows]
                turned.append(jnp.concatenate([yr * tr - yi * ti, yr * ti + yi * tr], axis=1))
        high, low = split(jnp.concatenate(turned, axis=0))
        flip = (((1,), (1,)), ((), ()))
        wide = dot(b_ref[...], high, flip)
        outer = wide[:256] + wide[256:] + dot(b_ref[:256], low, flip)
        for i in range(2):
            k = 2 * pair + i
            for part in range(2):
                images[part][pl.ds(k, 128, stride=8), :] = outer[
                    part * 128 : (part + 1) * 128, i * LANES : (i + 1) * LANES
                ]


def range_transform(cells, even, tables):
    fixed = lambda *shape: pl.BlockSpec(shape, lambda g: (0,) * len(shape))
    images = pl.pallas_call(
        range_kernel,
        grid=(4,),
        in_specs=[
            pl.BlockSpec((32, 2, 2, 8, LANES), lambda g: (0, 0, 0, g, 0)),
            pl.BlockSpec((8, 128, LANES), lambda g: (g, 0, 0)),
            fixed(128, 128),
            fixed(128, 128),
            fixed(2, 128, LANES),
            fixed(512, 256),
        ],
        out_specs=[pl.BlockSpec((1, 128, 8, LANES), lambda g: (g, 0, 0, 0))] * 2,
        out_shape=[jax.ShapeDtypeStruct((4, 128, 8, LANES), F32)] * 2,
        compiler_params=pltpu.CompilerParams(vmem_limit_bytes=40 * 1024 * 1024),
        cost_estimate=pl.CostEstimate(flops=32 * S * 384 * 6, bytes_accessed=8 * 2**20, transcendentals=0),
        name="range",
    )(cells, even, *tables)
    return [image.transpose(0, 2, 1, 3).reshape(32, S) for image in images]


def ends_kernel(*refs):
    tail_ref, head_ref = refs[8:]
    for i, ref in enumerate(refs[:8]):
        out_ref, part, half = (tail_ref, head_ref)[i // 4], i // 2 % 2, i % 2
        out_ref[part, :, half * LANES : (half + 1) * LANES] = ref[...]


def block_ends(groups, phase_real, phase_imag):
    block = lambda rows, g: pl.BlockSpec((HALO, LANES), lambda i: (rows, g))
    return pl.pallas_call(
        ends_kernel,
        grid=(1,),
        in_specs=[block(rows, g) for rows in (AZ // HALO - 1, 0) for part in range(2) for g in groups],
        out_specs=[pl.BlockSpec((2, HALO, 2 * LANES), lambda i: (0, 0, 0))] * 2,
        out_shape=[jax.ShapeDtypeStruct((2, HALO, 2 * LANES), F32)] * 2,
        compiler_params=pltpu.CompilerParams(vmem_limit_bytes=60 * 1024 * 1024),
        cost_estimate=pl.CostEstimate(flops=0, bytes_accessed=2 * 2**20, transcendentals=0),
        name="ends",
    )(*[phase_real, phase_real, phase_imag, phase_imag] * 2)


def resampling_weights(interp_tiles, tile_index, tile_count):
    tiles_dev = interp_tiles.shape[0]
    first_block = lax.axis_index("pulse") * tiles_dev
    offsets = tile_index - (first_block + jnp.arange(tiles_dev, dtype=jnp.int32))[:, None]
    live = jnp.arange(SLOTS, dtype=jnp.int32)[None, :] < tile_count[:, None]
    places = jnp.arange(-2, 3, dtype=jnp.int32)
    chosen = ((offsets[:, None, :] == places[None, :, None]) & live[:, None, :]).astype(F32)
    weights = jnp.sum(interp_tiles[:, None] * chosen[:, :, :, None, None], axis=2)
    weights = weights.reshape(tiles_dev, SLOTS, 32, 4, BLOCK).transpose(0, 3, 2, 1, 4)
    weights = weights.reshape(tiles_dev, BLOCK, SLOTS * BLOCK)
    high = lax.reduce_precision(weights, 8, 7)
    return high.astype(BF16), (weights - high).astype(BF16)


def shards(phase_real, phase_imag, interp_tiles, tile_index, tile_count):
    count = lax.axis_size("pulse")
    up = [(i, i + 1) for i in range(count - 1)]
    down = [(i + 1, i) for i in range(count - 1)]
    weights = resampling_weights(interp_tiles, tile_index, tile_count)
    tables = azimuth_tables()
    me = lax.axis_index("pulse")
    ends = []
    for groups in CHUNKS:
        tail, head = block_ends(groups, phase_real, phase_imag)
        if groups != CHUNKS[-1]:
            phase_real, phase_imag, tail, head = lax.optimization_barrier((phase_real, phase_imag, tail, head))
            ends.append((lax.ppermute(tail, "pulse", up), lax.ppermute(head, "pulse", down)))
            continue
        relayed = lax.ppermute(jnp.where(me == 2, head, tail), "pulse", [(2, 0), (5, 7)])
        relayed = lax.ppermute(relayed, "pulse", [(0, 1), (7, 6)])
        top = lax.ppermute(tail, "pulse", [pair for pair in up if pair != (5, 6)])
        bot = lax.ppermute(head, "pulse", [pair for pair in down if pair != (2, 1)])
        ends.append((jnp.where(me == 6, relayed, top), jnp.where(me == 1, relayed, bot)))
    cells = []
    for groups, (top, bot) in zip(CHUNKS, ends):
        sent = azimuth(groups, groups == CHUNKS[-1], phase_real, phase_imag, top, bot, weights, tables)
        cells.append(lax.all_to_all(sent, "range", split_axis=0, concat_axis=0, tiled=True))
    even, rest = range_tables()
    return tuple(range_transform(cells[1], even_blocks(cells[0], even), rest))


def solution(mesh):
    placed = (
        P("pulse", "range"),
        P("pulse", "range"),
        P("pulse", None, None, None),
        P("pulse", None),
        P("pulse"),
    )
    return jax.shard_map(
        shards,
        mesh=mesh,
        in_specs=placed,
        out_specs=(P(("pulse", "range"), None), P(("pulse", "range"), None)),
        check_vma=False,
    )
```

```python
import functools
import math

import jax
import jax.numpy as jnp
import ml_dtypes
import numpy as np
from jax import lax
from jax.experimental import pallas as pl
from jax.experimental.pallas import tpu as pltpu
from jax.sharding import PartitionSpec as P

S = 16384
AZ = 1024
BLOCK = 128
SLOTS = 5
HALO = 2 * BLOCK
LANES = 128
PARTS = (2, 2)
GROUPS = 4
RELAYS = (
    ((1, ()), (1, ((2, 0, 1), (5, 7, 6), (1, 3, 2), (6, 4, 5)))),
    ((2, ((2, 0, 1), (5, 7, 6), (3, 5, 4), (4, 2, 3))),),
)
BF16 = jnp.bfloat16
F32 = jnp.float32


def unit_roots(numerators, length):
    angles = 2.0 * math.pi * (numerators % length) / length
    return np.cos(angles), -np.sin(angles)


def halves(table):
    high = table.astype(ml_dtypes.bfloat16)
    low = (table - high.astype(np.float64)).astype(ml_dtypes.bfloat16)
    return high, low


def azimuth_tables():
    idx = np.arange(256)
    real, imag = unit_roots(idx[:, None] * idx[None, :], 256)
    high, low = halves(np.concatenate([real, imag], axis=0) / 32.0)
    turns = []
    for a in range(1, 4):
        turn = np.stack(unit_roots(a * idx, 1024))
        turns.append(np.broadcast_to(turn[:, :, None], (2, 256, LANES)))
    return high, low, np.stack(turns).astype(np.float32)


def range_tables(parts):
    idx = np.arange(128)
    order = []
    first = 0
    for width in parts:
        for source in range(32):
            order += [4 * source + first + c for c in range(width)]
        first += width
    order = np.array(order)
    real, imag = unit_roots(idx[:, None] * order[None, :], 128)
    inner = np.block([[real, -imag], [imag, real]])
    turn = np.stack(unit_roots(idx[:, None] * idx[None, :], S)).astype(np.float32)
    real, imag = unit_roots(idx[:, None] * idx[None, :], 128)
    outer = np.block([[real, -imag], [imag, real]]) / 128.0
    return (*halves(inner), turn, *halves(outer))


def split(value):
    high = value.astype(BF16)
    return high, (value - high.astype(F32)).astype(BF16)


def dot(a, b, dims=(((1,), (0,)), ((), ()))):
    return lax.dot_general(a, b, dims, preferred_element_type=F32)


def azimuth_kernel(re_ref, im_ref, top_ref, bot_ref, wh_ref, wl_ref, dh_ref, dl_ref, tw_ref, out_ref, xh, xl, yh, yl):
    def put(row, real, imag):
        high, low = split(jnp.concatenate([real, imag], axis=1))
        xh[row : row + BLOCK, :] = high
        xl[row : row + BLOCK, :] = low

    for i in range(2):
        rows = slice(i * BLOCK, (i + 1) * BLOCK)
        put(i * BLOCK, top_ref[0, rows], top_ref[1, rows])
        put(HALO + AZ + i * BLOCK, bot_ref[0, rows], bot_ref[1, rows])
    for i in range(AZ // BLOCK):
        rows = slice(i * BLOCK, (i + 1) * BLOCK)
        put(HALO + i * BLOCK, re_ref[rows], im_ref[rows])
    for b in range(AZ // BLOCK):
        rows = slice(b * BLOCK, (b + SLOTS) * BLOCK)
        cells = dot(wh_ref[b], xh[rows]) + dot(wl_ref[b], xh[rows]) + dot(wh_ref[b], xl[rows])
        high, low = split(cells)
        for a in range(4):
            yh[a, b * 32 : (b + 1) * 32] = high[a * 32 : (a + 1) * 32]
            yl[a, b * 32 : (b + 1) * 32] = low[a * 32 : (a + 1) * 32]
    real, imag = [], []
    for a in range(4):
        four = dot(dh_ref[...], yh[a]) + dot(dl_ref[...], yh[a]) + dot(dh_ref[...], yl[a])
        vr = four[:256, :LANES] - four[256:, LANES:]
        vi = four[:256, LANES:] + four[256:, :LANES]
        if a:
            tr, ti = tw_ref[a - 1, 0], tw_ref[a - 1, 1]
            vr, vi = vr * tr - vi * ti, vr * ti + vi * tr
        real.append(vr)
        imag.append(vi)
    er, ei, fr, fi = real[0] + real[2], imag[0] + imag[2], real[0] - real[2], imag[0] - imag[2]
    gr, gi, hr, hi = real[1] + real[3], imag[1] + imag[3], real[1] - real[3], imag[1] - imag[3]
    bins = [(er + gr, ei + gi), (fr + hi, fi - hr), (er - gr, ei - gi), (fr - hi, fi + hr)]
    for quarter in range(4):
        for part in range(2):
            for t in range(8):
                out_ref[quarter * 8 + t, 0, part] = bins[quarter][part][t * 32 : (t + 1) * 32]


def azimuth(first, width, phase_real, phase_imag, top, bot, weights, tables):
    fixed = lambda *shape: pl.BlockSpec(shape, lambda i: (0,) * len(shape))
    return pl.pallas_call(
        azimuth_kernel,
        grid=(width,),
        in_specs=[
            pl.BlockSpec((AZ, LANES), lambda i: (0, first + i)),
            pl.BlockSpec((AZ, LANES), lambda i: (0, first + i)),
            pl.BlockSpec((2, HALO, LANES), lambda i: (0, 0, i)),
            pl.BlockSpec((2, HALO, LANES), lambda i: (0, 0, i)),
            fixed(8, BLOCK, SLOTS * BLOCK),
            fixed(8, BLOCK, SLOTS * BLOCK),
            fixed(512, 256),
            fixed(512, 256),
            fixed(3, 2, 256, LANES),
        ],
        out_specs=pl.BlockSpec((32, 1, 2, 32, LANES), lambda i: (0, i, 0, 0, 0)),
        out_shape=jax.ShapeDtypeStruct((32, width, 2, 32, LANES), F32),
        scratch_shapes=[
            pltpu.VMEM((AZ + 2 * HALO, 2 * LANES), BF16),
            pltpu.VMEM((AZ + 2 * HALO, 2 * LANES), BF16),
            pltpu.VMEM((4, 256, 2 * LANES), BF16),
            pltpu.VMEM((4, 256, 2 * LANES), BF16),
        ],
        compiler_params=pltpu.CompilerParams(vmem_limit_bytes=40 * 1024 * 1024),
        cost_estimate=pl.CostEstimate(
            flops=6 * width * 256 * (AZ * 640 + AZ * 512) * (100 if first else 1), bytes_accessed=width * 2 * 2**20, transcendentals=0
        ),
        name="azimuth",
    )(phase_real, phase_imag, top, bot, *weights, *tables)


def range_kernel(parts, *refs):
    cells = refs[: len(parts)]
    ah_ref, al_ref, tw_ref, bh_ref, bl_ref, re_ref, im_ref = refs[len(parts) :]
    images = [ref.reshape(128 * 8, LANES) for ref in (re_ref, im_ref)]
    inner_table = jnp.concatenate([ah_ref[...], al_ref[...], ah_ref[...]], axis=1)
    outer_table = jnp.concatenate([bh_ref[...], bl_ref[...]], axis=0)
    flat = [ref.reshape(32 * width * 16, LANES) for ref, width in zip(cells, parts)]

    def rows_of(part, k):
        return jnp.concatenate(
            [ref[pl.ds(part * 8 + k, 32 * width, stride=16), :] for ref, width in zip(flat, parts)], axis=0
        )

    tr, ti = tw_ref[0], tw_ref[1]
    for pair in range(4):
        k0, k1 = 2 * pair, 2 * pair + 1
        full = jnp.concatenate(
            [jnp.concatenate([rows_of(part, k) for k in (k0, k1)], axis=1) for part in range(2)], axis=0
        )
        high, low = split(full)
        inner = dot(inner_table, jnp.concatenate([high, high, low], axis=0))
        turned = []
        for i in range(2):
            yr, yi = inner[:128, i * LANES : (i + 1) * LANES], inner[128:, i * LANES : (i + 1) * LANES]
            turned.append(jnp.concatenate([yr * tr - yi * ti, yr * ti + yi * tr], axis=1))
        high, low = split(jnp.concatenate(turned, axis=0))
        flip = (((1,), (1,)), ((), ()))
        wide = dot(outer_table, high, flip)
        outer = wide[:256] + wide[256:] + dot(bh_ref[...], low, flip)
        for i, k in enumerate((k0, k1)):
            for part in range(2):
                images[part][pl.ds(k, 128, stride=8), :] = outer[
                    part * 128 : (part + 1) * 128, i * LANES : (i + 1) * LANES
                ]


def range_transform(parts, cells, tables):
    fixed = lambda *shape: pl.BlockSpec(shape, lambda g: (0,) * len(shape))
    images = pl.pallas_call(
        functools.partial(range_kernel, parts),
        grid=(4,),
        in_specs=[pl.BlockSpec((32, width, 2, 8, LANES), lambda g: (0, 0, 0, g, 0)) for width in parts]
        + [fixed(256, 256), fixed(256, 256), fixed(2, 128, LANES), fixed(256, 256), fixed(256, 256)],
        out_specs=[pl.BlockSpec((1, 128, 8, LANES), lambda g: (g, 0, 0, 0))] * 2,
        out_shape=[jax.ShapeDtypeStruct((4, 128, 8, LANES), F32)] * 2,
        compiler_params=pltpu.CompilerParams(vmem_limit_bytes=40 * 1024 * 1024),
        cost_estimate=pl.CostEstimate(flops=4 * 32 * S * 256 * 3, bytes_accessed=8 * 2**20, transcendentals=0),
        name="range",
    )(*cells, *tables)
    return [image.transpose(0, 2, 1, 3).reshape(32, S) for image in images]


def resampling_weights(interp_tiles, tile_index, tile_count):
    tiles_dev = interp_tiles.shape[0]
    first_block = lax.axis_index("pulse") * tiles_dev
    offsets = tile_index - (first_block + jnp.arange(tiles_dev, dtype=jnp.int32))[:, None]
    live = jnp.arange(SLOTS, dtype=jnp.int32)[None, :] < tile_count[:, None]
    places = jnp.arange(-2, 3, dtype=jnp.int32)
    chosen = ((offsets[:, None, :] == places[None, :, None]) & live[:, None, :]).astype(F32)
    weights = jnp.sum(interp_tiles[:, None] * chosen[:, :, :, None, None], axis=2)
    weights = weights.reshape(tiles_dev, SLOTS, 32, 4, BLOCK).transpose(0, 3, 2, 1, 4)
    weights = weights.reshape(tiles_dev, BLOCK, SLOTS * BLOCK)
    high = lax.reduce_precision(weights, 8, 7)
    return high.astype(BF16), (weights - high).astype(BF16)


def shards(phase_real, phase_imag, interp_tiles, tile_index, tile_count):
    count = lax.axis_size("pulse")
    up = [(i, i + 1) for i in range(count - 1)]
    down = [(i + 1, i) for i in range(count - 1)]
    weights = resampling_weights(interp_tiles, tile_index, tile_count)
    tables = azimuth_tables()
    me = lax.axis_index("pulse")
    even = me % 2 == 0

    def rows_of(first, width):
        columns = slice(first * LANES, (first + width) * LANES)
        tail = jnp.stack([phase_real[AZ - HALO :, columns], phase_imag[AZ - HALO :, columns]])
        head = jnp.stack([phase_real[:HALO, columns], phase_imag[:HALO, columns]])
        return tail, head

    def exchange(first, width, relays):
        tail, head = rows_of(first, width)
        away = [(a, c) for a, b, c in relays]
        top = lax.ppermute(tail, "pulse", [pair for pair in up if pair not in away])
        bot = lax.ppermute(head, "pulse", [pair for pair in down if pair not in away])
        if relays:
            passed = lax.ppermute(jnp.where(even, head, tail), "pulse", [(a, b) for a, b, c in relays])
            passed = lax.ppermute(passed, "pulse", [(b, c) for a, b, c in relays])
            top, bot = jnp.where(even, top + passed, top), jnp.where(even, bot, bot + passed)
        return top, bot

    ends = []
    first = 0
    for chunk in RELAYS:
        parts = []
        for width, relays in chunk:
            parts.append(exchange(first, width, relays))
            first += width
        ends.append([jnp.concatenate(side, axis=2) if len(side) > 1 else side[0] for side in zip(*parts)])
    cells = []
    first = 0
    for width, (top, bot) in zip(PARTS, ends):
        sent = azimuth(first, width, phase_real, phase_imag, top, bot, weights, tables)
        cells.append(lax.all_to_all(sent, "range", split_axis=0, concat_axis=0, tiled=True))
        first += width
    return tuple(range_transform(PARTS, cells, range_tables(PARTS)))


def solution(mesh):
    placed = (
        P("pulse", "range"),
        P("pulse", "range"),
        P("pulse", None, None, None),
        P("pulse", None),
        P("pulse"),
    )
    return jax.shard_map(
        shards,
        mesh=mesh,
        in_specs=placed,
        out_specs=(P(("pulse", "range"), None), P(("pulse", "range"), None)),
        check_vma=False,
    )
```

```python
import functools
import math

import jax
import jax.numpy as jnp
import ml_dtypes
import numpy as np
from jax import lax
from jax.experimental import pallas as pl
from jax.experimental.pallas import tpu as pltpu
from jax.sharding import PartitionSpec as P

S = 16384
AZ = 1024
BLOCK = 128
SLOTS = 5
HALO = 2 * BLOCK
LANES = 128
PARTS = (2, 2)
GROUPS = 4
ALL = tuple(range(32))
ONE_CORE = tuple(range(0, 32, 2))
MIDDLE = tuple(r for r in ONE_CORE if r // 8 in (1, 2))
RELAYS = (
    (2, 0, 1, ALL),
    (5, 7, 6, ALL),
    (3, 5, 4, ONE_CORE),
    (4, 2, 3, ONE_CORE),
    (1, 3, 2, MIDDLE),
    (6, 4, 5, MIDDLE),
)
BF16 = jnp.bfloat16
F32 = jnp.float32


def unit_roots(numerators, length):
    angles = 2.0 * math.pi * (numerators % length) / length
    return np.cos(angles), -np.sin(angles)


def halves(table):
    high = table.astype(ml_dtypes.bfloat16)
    low = (table - high.astype(np.float64)).astype(ml_dtypes.bfloat16)
    return high, low


def azimuth_tables():
    idx = np.arange(256)
    real, imag = unit_roots(idx[:, None] * idx[None, :], 256)
    high, low = halves(np.concatenate([real, imag], axis=0) / 32.0)
    turns = []
    for a in range(1, 4):
        turn = np.stack(unit_roots(a * idx, 1024))
        turns.append(np.broadcast_to(turn[:, :, None], (2, 256, LANES)))
    return high, low, np.stack(turns).astype(np.float32)


def range_tables(parts):
    idx = np.arange(128)
    order = []
    first = 0
    for width in parts:
        for source in range(32):
            order += [4 * source + first + c for c in range(width)]
        first += width
    order = np.array(order)
    real, imag = unit_roots(idx[:, None] * order[None, :], 128)
    inner = np.block([[real, -imag], [imag, real]])
    turn = np.stack(unit_roots(idx[:, None] * idx[None, :], S)).astype(np.float32)
    real, imag = unit_roots(idx[:, None] * idx[None, :], 128)
    outer = np.block([[real, -imag], [imag, real]]) / 128.0
    return (*halves(inner), turn, *halves(outer))


def split(value):
    high = value.astype(BF16)
    return high, (value - high.astype(F32)).astype(BF16)


def dot(a, b, dims=(((1,), (0,)), ((), ()))):
    return lax.dot_general(a, b, dims, preferred_element_type=F32)


def azimuth_kernel(re_ref, im_ref, top_ref, bot_ref, wh_ref, wl_ref, dh_ref, dl_ref, tw_ref, out_ref, xh, xl, yh, yl):
    def put(row, real, imag):
        high, low = split(jnp.concatenate([real, imag], axis=1))
        xh[row : row + BLOCK, :] = high
        xl[row : row + BLOCK, :] = low

    for i in range(2):
        rows = slice(i * BLOCK, (i + 1) * BLOCK)
        put(i * BLOCK, top_ref[0, rows], top_ref[1, rows])
        put(HALO + AZ + i * BLOCK, bot_ref[0, rows], bot_ref[1, rows])
    for i in range(AZ // BLOCK):
        rows = slice(i * BLOCK, (i + 1) * BLOCK)
        put(HALO + i * BLOCK, re_ref[rows], im_ref[rows])
    for b in range(AZ // BLOCK):
        rows = slice(b * BLOCK, (b + SLOTS) * BLOCK)
        cells = dot(wh_ref[b], xh[rows]) + dot(wl_ref[b], xh[rows]) + dot(wh_ref[b], xl[rows])
        high, low = split(cells)
        for a in range(4):
            yh[a, b * 32 : (b + 1) * 32] = high[a * 32 : (a + 1) * 32]
            yl[a, b * 32 : (b + 1) * 32] = low[a * 32 : (a + 1) * 32]
    real, imag = [], []
    for a in range(4):
        four = dot(dh_ref[...], yh[a]) + dot(dl_ref[...], yh[a]) + dot(dh_ref[...], yl[a])
        vr = four[:256, :LANES] - four[256:, LANES:]
        vi = four[:256, LANES:] + four[256:, :LANES]
        if a:
            tr, ti = tw_ref[a - 1, 0], tw_ref[a - 1, 1]
            vr, vi = vr * tr - vi * ti, vr * ti + vi * tr
        real.append(vr)
        imag.append(vi)
    er, ei, fr, fi = real[0] + real[2], imag[0] + imag[2], real[0] - real[2], imag[0] - imag[2]
    gr, gi, hr, hi = real[1] + real[3], imag[1] + imag[3], real[1] - real[3], imag[1] - imag[3]
    bins = [(er + gr, ei + gi), (fr + hi, fi - hr), (er - gr, ei - gi), (fr - hi, fi + hr)]
    for quarter in range(4):
        for part in range(2):
            for t in range(8):
                out_ref[quarter * 8 + t, 0, part] = bins[quarter][part][t * 32 : (t + 1) * 32]


def azimuth(first, width, phase_real, phase_imag, top, bot, weights, tables):
    fixed = lambda *shape: pl.BlockSpec(shape, lambda i: (0,) * len(shape))
    return pl.pallas_call(
        azimuth_kernel,
        grid=(width,),
        in_specs=[
            pl.BlockSpec((AZ, LANES), lambda i: (0, first + i)),
            pl.BlockSpec((AZ, LANES), lambda i: (0, first + i)),
            pl.BlockSpec((2, HALO, LANES), lambda i: (0, 0, i)),
            pl.BlockSpec((2, HALO, LANES), lambda i: (0, 0, i)),
            fixed(8, BLOCK, SLOTS * BLOCK),
            fixed(8, BLOCK, SLOTS * BLOCK),
            fixed(512, 256),
            fixed(512, 256),
            fixed(3, 2, 256, LANES),
        ],
        out_specs=pl.BlockSpec((32, 1, 2, 32, LANES), lambda i: (0, i, 0, 0, 0)),
        out_shape=jax.ShapeDtypeStruct((32, width, 2, 32, LANES), F32),
        scratch_shapes=[
            pltpu.VMEM((AZ + 2 * HALO, 2 * LANES), BF16),
            pltpu.VMEM((AZ + 2 * HALO, 2 * LANES), BF16),
            pltpu.VMEM((4, 256, 2 * LANES), BF16),
            pltpu.VMEM((4, 256, 2 * LANES), BF16),
        ],
        compiler_params=pltpu.CompilerParams(vmem_limit_bytes=40 * 1024 * 1024),
        cost_estimate=pl.CostEstimate(
            flops=6 * width * 256 * (AZ * 640 + AZ * 512) * (100 if first else 1), bytes_accessed=width * 2 * 2**20, transcendentals=0
        ),
        name="azimuth",
    )(phase_real, phase_imag, top, bot, *weights, *tables)


def range_kernel(parts, *refs):
    cells = refs[: len(parts)]
    ah_ref, al_ref, tw_ref, bh_ref, bl_ref, re_ref, im_ref = refs[len(parts) :]
    images = [ref.reshape(128 * 8, LANES) for ref in (re_ref, im_ref)]
    inner_table = jnp.concatenate([ah_ref[...], al_ref[...], ah_ref[...]], axis=1)
    outer_table = jnp.concatenate([bh_ref[...], bl_ref[...]], axis=0)
    flat = [ref.reshape(32 * width * 16, LANES) for ref, width in zip(cells, parts)]

    def rows_of(part, k):
        return jnp.concatenate(
            [ref[pl.ds(part * 8 + k, 32 * width, stride=16), :] for ref, width in zip(flat, parts)], axis=0
        )

    tr, ti = tw_ref[0], tw_ref[1]
    for pair in range(4):
        k0, k1 = 2 * pair, 2 * pair + 1
        full = jnp.concatenate(
            [jnp.concatenate([rows_of(part, k) for k in (k0, k1)], axis=1) for part in range(2)], axis=0
        )
        high, low = split(full)
        inner = dot(inner_table, jnp.concatenate([high, high, low], axis=0))
        turned = []
        for i in range(2):
            yr, yi = inner[:128, i * LANES : (i + 1) * LANES], inner[128:, i * LANES : (i + 1) * LANES]
            turned.append(jnp.concatenate([yr * tr - yi * ti, yr * ti + yi * tr], axis=1))
        high, low = split(jnp.concatenate(turned, axis=0))
        flip = (((1,), (1,)), ((), ()))
        wide = dot(outer_table, high, flip)
        outer = wide[:256] + wide[256:] + dot(bh_ref[...], low, flip)
        for i, k in enumerate((k0, k1)):
            for part in range(2):
                images[part][pl.ds(k, 128, stride=8), :] = outer[
                    part * 128 : (part + 1) * 128, i * LANES : (i + 1) * LANES
                ]


def range_transform(parts, cells, tables):
    fixed = lambda *shape: pl.BlockSpec(shape, lambda g: (0,) * len(shape))
    images = pl.pallas_call(
        functools.partial(range_kernel, parts),
        grid=(4,),
        in_specs=[pl.BlockSpec((32, width, 2, 8, LANES), lambda g: (0, 0, 0, g, 0)) for width in parts]
        + [fixed(256, 256), fixed(256, 256), fixed(2, 128, LANES), fixed(256, 256), fixed(256, 256)],
        out_specs=[pl.BlockSpec((1, 128, 8, LANES), lambda g: (g, 0, 0, 0))] * 2,
        out_shape=[jax.ShapeDtypeStruct((4, 128, 8, LANES), F32)] * 2,
        compiler_params=pltpu.CompilerParams(vmem_limit_bytes=40 * 1024 * 1024),
        cost_estimate=pl.CostEstimate(flops=4 * 32 * S * 256 * 3, bytes_accessed=8 * 2**20, transcendentals=0),
        name="range",
    )(*cells, *tables)
    return [image.transpose(0, 2, 1, 3).reshape(32, S) for image in images]


def resampling_weights(interp_tiles, tile_index, tile_count):
    tiles_dev = interp_tiles.shape[0]
    first_block = lax.axis_index("pulse") * tiles_dev
    offsets = tile_index - (first_block + jnp.arange(tiles_dev, dtype=jnp.int32))[:, None]
    live = jnp.arange(SLOTS, dtype=jnp.int32)[None, :] < tile_count[:, None]
    places = jnp.arange(-2, 3, dtype=jnp.int32)
    chosen = ((offsets[:, None, :] == places[None, :, None]) & live[:, None, :]).astype(F32)
    weights = jnp.sum(interp_tiles[:, None] * chosen[:, :, :, None, None], axis=2)
    weights = weights.reshape(tiles_dev, SLOTS, 32, 4, BLOCK).transpose(0, 3, 2, 1, 4)
    weights = weights.reshape(tiles_dev, BLOCK, SLOTS * BLOCK)
    high = lax.reduce_precision(weights, 8, 7)
    return high.astype(BF16), (weights - high).astype(BF16)


def shards(phase_real, phase_imag, interp_tiles, tile_index, tile_count):
    count = lax.axis_size("pulse")
    up = [(i, i + 1) for i in range(count - 1)]
    down = [(i + 1, i) for i in range(count - 1)]
    weights = resampling_weights(interp_tiles, tile_index, tile_count)
    tables = azimuth_tables()
    even = lax.axis_index("pulse") % 2 == 0
    ends = []
    first = 0
    for width in PARTS:
        columns = slice(first * LANES, (first + width) * LANES)
        tail = jnp.stack([phase_real[AZ - HALO :, columns], phase_imag[AZ - HALO :, columns]])
        head = jnp.stack([phase_real[:HALO, columns], phase_imag[:HALO, columns]])
        first += width
        if first < GROUPS:
            phase_real, phase_imag, tail, head = lax.optimization_barrier((phase_real, phase_imag, tail, head))
            ends.append((lax.ppermute(tail, "pulse", up), lax.ppermute(head, "pulse", down)))
            continue
        away = {(a, c): ranks for a, b, c, ranks in RELAYS}
        ways = [
            [(32 * a + r, 32 * b + r) for a, b in pairs for r in range(32) if r not in away.get((a, b), ())]
            for pairs in (up, down)
        ]
        hops = [
            [(32 * legs[k] + r, 32 * legs[k + 1] + r) for *legs, ranks in RELAYS for r in ranks] for k in range(2)
        ]
        both = ("pulse", "range")
        top, bot = lax.ppermute(tail, both, ways[0]), lax.ppermute(head, both, ways[1])
        passed = lax.ppermute(jnp.where(even, head, tail), both, hops[0])
        passed = lax.ppermute(passed, both, hops[1])
        ends.append((jnp.where(even, top + passed, top), jnp.where(even, bot, bot + passed)))
    cells = []
    first = 0
    for width, (top, bot) in zip(PARTS, ends):
        sent = azimuth(first, width, phase_real, phase_imag, top, bot, weights, tables)
        cells.append(lax.all_to_all(sent, "range", split_axis=0, concat_axis=0, tiled=True))
        first += width
    return tuple(range_transform(PARTS, cells, range_tables(PARTS)))


def solution(mesh):
    placed = (
        P("pulse", "range"),
        P("pulse", "range"),
        P("pulse", None, None, None),
        P("pulse", None),
        P("pulse"),
    )
    return jax.shard_map(
        shards,
        mesh=mesh,
        in_specs=placed,
        out_specs=(P(("pulse", "range"), None), P(("pulse", "range"), None)),
        check_vma=False,
    )
```

```python
import functools
import math

import jax
import jax.numpy as jnp
import ml_dtypes
import numpy as np
from jax import lax
from jax.experimental import pallas as pl
from jax.experimental.pallas import tpu as pltpu
from jax.sharding import PartitionSpec as P

S = 16384
AZ = 1024
BLOCK = 128
SLOTS = 5
HALO = 2 * BLOCK
LANES = 128
PARTS = (2, 2)
GROUPS = 4
ALL = tuple(range(32))
ONE_CORE = tuple(range(0, 32, 2))
MOST = tuple(r for r in range(32) if r % 2 == 0 or r // 8 in (1, 2))
MIDDLE = tuple(r for r in ONE_CORE if r // 8 in (1, 2))
RELAYS = (
    (2, 0, 1, ALL),
    (5, 7, 6, ALL),
    (3, 5, 4, MOST),
    (4, 2, 3, MOST),
    (1, 3, 2, MIDDLE),
    (6, 4, 5, MIDDLE),
)
BF16 = jnp.bfloat16
F32 = jnp.float32


def unit_roots(numerators, length):
    angles = 2.0 * math.pi * (numerators % length) / length
    return np.cos(angles), -np.sin(angles)


def halves(table):
    high = table.astype(ml_dtypes.bfloat16)
    low = (table - high.astype(np.float64)).astype(ml_dtypes.bfloat16)
    return high, low


def azimuth_tables():
    idx = np.arange(256)
    real, imag = unit_roots(idx[:, None] * idx[None, :], 256)
    high, low = halves(np.concatenate([real, imag], axis=0) / 32.0)
    turns = []
    for a in range(1, 4):
        turn = np.stack(unit_roots(a * idx, 1024))
        turns.append(np.broadcast_to(turn[:, :, None], (2, 256, LANES)))
    return high, low, np.stack(turns).astype(np.float32)


def range_tables(parts):
    idx = np.arange(128)
    order = []
    first = 0
    for width in parts:
        for source in range(32):
            order += [4 * source + first + c for c in range(width)]
        first += width
    order = np.array(order)
    real, imag = unit_roots(idx[:, None] * order[None, :], 128)
    inner = np.block([[real, -imag], [imag, real]])
    turn = np.stack(unit_roots(idx[:, None] * idx[None, :], S)).astype(np.float32)
    real, imag = unit_roots(idx[:, None] * idx[None, :], 128)
    outer = np.block([[real, -imag], [imag, real]]) / 128.0
    return (*halves(inner), turn, *halves(outer))


def split(value):
    high = value.astype(BF16)
    return high, (value - high.astype(F32)).astype(BF16)


def dot(a, b, dims=(((1,), (0,)), ((), ()))):
    return lax.dot_general(a, b, dims, preferred_element_type=F32)


def own_kernel(re_ref, im_ref, wh_ref, wl_ref, out_ref, xh, xl):
    for i in range(AZ // BLOCK):
        rows = slice(i * BLOCK, (i + 1) * BLOCK)
        xh[rows], xl[rows] = split(jnp.concatenate([re_ref[rows], im_ref[rows]], axis=1))
    for b in range(AZ // BLOCK):
        low, high = max(b - 2, 0), min(b + 3, AZ // BLOCK)
        rows = slice(low * BLOCK, high * BLOCK)
        slots = slice((low - b + 2) * BLOCK, (high - b + 2) * BLOCK)
        wh, wl = wh_ref[b, :, slots], wl_ref[b, :, slots]
        out_ref[0, b * BLOCK : (b + 1) * BLOCK] = dot(wh, xh[rows]) + dot(wl, xh[rows]) + dot(wh, xl[rows])


def own_part(phase_real, phase_imag, weights):
    tile = pl.BlockSpec((8, BLOCK, SLOTS * BLOCK), lambda i: (0, 0, 0))
    return pl.pallas_call(
        own_kernel,
        grid=(GROUPS,),
        in_specs=[pl.BlockSpec((AZ, LANES), lambda i: (0, i))] * 2 + [tile, tile],
        out_specs=pl.BlockSpec((1, AZ, 2 * LANES), lambda i: (i, 0, 0)),
        out_shape=jax.ShapeDtypeStruct((GROUPS, AZ, 2 * LANES), F32),
        scratch_shapes=[pltpu.VMEM((AZ, 2 * LANES), BF16)] * 2,
        compiler_params=pltpu.CompilerParams(vmem_limit_bytes=40 * 1024 * 1024),
        cost_estimate=pl.CostEstimate(flops=1, bytes_accessed=1, transcendentals=0),
        name="own",
    )(phase_real, phase_imag, *weights)


def edge_weights(weights):
    none = jnp.zeros((BLOCK, BLOCK), weights.dtype)
    before = [weights[0, :, : 2 * BLOCK], jnp.concatenate([none, weights[1, :, :BLOCK]], axis=1)]
    after = [jnp.concatenate([weights[6, :, 4 * BLOCK :], none], axis=1), weights[7, :, 3 * BLOCK :]]
    return jnp.stack([jnp.concatenate(before, axis=0), jnp.concatenate(after, axis=0)])


def azimuth_kernel(own_ref, top_ref, bot_ref, wh_ref, wl_ref, dh_ref, dl_ref, tw_ref, out_ref, yh, yl):
    def put(row, cells):
        high, low = split(cells)
        for b in range(2):
            for a in range(4):
                rows = slice(b * BLOCK + a * 32, b * BLOCK + (a + 1) * 32)
                place = row // 4 + b * 32
                yh[a, place : place + 32] = high[rows]
                yl[a, place : place + 32] = low[rows]

    for side, (row, ref) in enumerate(((0, top_ref), (AZ - HALO, bot_ref))):
        high, low = split(jnp.concatenate([ref[0], ref[1]], axis=1))
        wh, wl = wh_ref[side], wl_ref[side]
        put(row, own_ref[0, row : row + HALO] + (dot(wh, high) + dot(wl, high) + dot(wh, low)))
    for row in range(HALO, AZ - HALO, HALO):
        put(row, own_ref[0, row : row + HALO])
    real, imag = [], []
    for a in range(4):
        four = dot(dh_ref[...], yh[a]) + dot(dl_ref[...], yh[a]) + dot(dh_ref[...], yl[a])
        vr = four[:256, :LANES] - four[256:, LANES:]
        vi = four[:256, LANES:] + four[256:, :LANES]
        if a:
            tr, ti = tw_ref[a - 1, 0], tw_ref[a - 1, 1]
            vr, vi = vr * tr - vi * ti, vr * ti + vi * tr
        real.append(vr)
        imag.append(vi)
    er, ei, fr, fi = real[0] + real[2], imag[0] + imag[2], real[0] - real[2], imag[0] - imag[2]
    gr, gi, hr, hi = real[1] + real[3], imag[1] + imag[3], real[1] - real[3], imag[1] - imag[3]
    bins = [(er + gr, ei + gi), (fr + hi, fi - hr), (er - gr, ei - gi), (fr - hi, fi + hr)]
    for quarter in range(4):
        for part in range(2):
            for t in range(8):
                out_ref[quarter * 8 + t, 0, part] = bins[quarter][part][t * 32 : (t + 1) * 32]


def azimuth(first, width, own, top, bot, weights, tables):
    fixed = lambda *shape: pl.BlockSpec(shape, lambda i: (0,) * len(shape))
    return pl.pallas_call(
        azimuth_kernel,
        grid=(width,),
        in_specs=[
            pl.BlockSpec((1, AZ, 2 * LANES), lambda i: (first + i, 0, 0)),
            pl.BlockSpec((2, HALO, LANES), lambda i: (0, 0, i)),
            pl.BlockSpec((2, HALO, LANES), lambda i: (0, 0, i)),
            fixed(2, HALO, HALO),
            fixed(2, HALO, HALO),
            fixed(512, 256),
            fixed(512, 256),
            fixed(3, 2, 256, LANES),
        ],
        out_specs=pl.BlockSpec((32, 1, 2, 32, LANES), lambda i: (0, i, 0, 0, 0)),
        out_shape=jax.ShapeDtypeStruct((32, width, 2, 32, LANES), F32),
        scratch_shapes=[pltpu.VMEM((4, 256, 2 * LANES), BF16)] * 2,
        compiler_params=pltpu.CompilerParams(vmem_limit_bytes=40 * 1024 * 1024),
        cost_estimate=pl.CostEstimate(
            flops=6 * width * 256 * AZ * 1152 * (100 if first else 1), bytes_accessed=width * 2**21, transcendentals=0
        ),
        name="azimuth",
    )(own, top, bot, *weights, *tables)


def range_kernel(parts, *refs):
    cells = refs[: len(parts)]
    ah_ref, al_ref, tw_ref, bh_ref, bl_ref, re_ref, im_ref = refs[len(parts) :]
    images = [ref.reshape(128 * 8, LANES) for ref in (re_ref, im_ref)]
    inner_table = jnp.concatenate([ah_ref[...], al_ref[...], ah_ref[...]], axis=1)
    outer_table = jnp.concatenate([bh_ref[...], bl_ref[...]], axis=0)
    flat = [ref.reshape(32 * width * 16, LANES) for ref, width in zip(cells, parts)]

    def rows_of(part, k):
        return jnp.concatenate(
            [ref[pl.ds(part * 8 + k, 32 * width, stride=16), :] for ref, width in zip(flat, parts)], axis=0
        )

    tr, ti = tw_ref[0], tw_ref[1]
    for pair in range(4):
        k0, k1 = 2 * pair, 2 * pair + 1
        full = jnp.concatenate(
            [jnp.concatenate([rows_of(part, k) for k in (k0, k1)], axis=1) for part in range(2)], axis=0
        )
        high, low = split(full)
        inner = dot(inner_table, jnp.concatenate([high, high, low], axis=0))
        turned = []
        for i in range(2):
            yr, yi = inner[:128, i * LANES : (i + 1) * LANES], inner[128:, i * LANES : (i + 1) * LANES]
            turned.append(jnp.concatenate([yr * tr - yi * ti, yr * ti + yi * tr], axis=1))
        high, low = split(jnp.concatenate(turned, axis=0))
        flip = (((1,), (1,)), ((), ()))
        wide = dot(outer_table, high, flip)
        outer = wide[:256] + wide[256:] + dot(bh_ref[...], low, flip)
        for i, k in enumerate((k0, k1)):
            for part in range(2):
                images[part][pl.ds(k, 128, stride=8), :] = outer[
                    part * 128 : (part + 1) * 128, i * LANES : (i + 1) * LANES
                ]


def range_transform(parts, cells, tables):
    fixed = lambda *shape: pl.BlockSpec(shape, lambda g: (0,) * len(shape))
    images = pl.pallas_call(
        functools.partial(range_kernel, parts),
        grid=(4,),
        in_specs=[pl.BlockSpec((32, width, 2, 8, LANES), lambda g: (0, 0, 0, g, 0)) for width in parts]
        + [fixed(256, 256), fixed(256, 256), fixed(2, 128, LANES), fixed(256, 256), fixed(256, 256)],
        out_specs=[pl.BlockSpec((1, 128, 8, LANES), lambda g: (g, 0, 0, 0))] * 2,
        out_shape=[jax.ShapeDtypeStruct((4, 128, 8, LANES), F32)] * 2,
        compiler_params=pltpu.CompilerParams(vmem_limit_bytes=40 * 1024 * 1024),
        cost_estimate=pl.CostEstimate(flops=4 * 32 * S * 256 * 3, bytes_accessed=8 * 2**20, transcendentals=0),
        name="range",
    )(*cells, *tables)
    return [image.transpose(0, 2, 1, 3).reshape(32, S) for image in images]


def resampling_weights(interp_tiles, tile_index, tile_count):
    tiles_dev = interp_tiles.shape[0]
    first_block = lax.axis_index("pulse") * tiles_dev
    offsets = tile_index - (first_block + jnp.arange(tiles_dev, dtype=jnp.int32))[:, None]
    live = jnp.arange(SLOTS, dtype=jnp.int32)[None, :] < tile_count[:, None]
    places = jnp.arange(-2, 3, dtype=jnp.int32)
    chosen = ((offsets[:, None, :] == places[None, :, None]) & live[:, None, :]).astype(F32)
    weights = jnp.sum(interp_tiles[:, None] * chosen[:, :, :, None, None], axis=2)
    weights = weights.reshape(tiles_dev, SLOTS, 32, 4, BLOCK).transpose(0, 3, 2, 1, 4)
    weights = weights.reshape(tiles_dev, BLOCK, SLOTS * BLOCK)
    high = lax.reduce_precision(weights, 8, 7)
    return high.astype(BF16), (weights - high).astype(BF16)


def shards(phase_real, phase_imag, interp_tiles, tile_index, tile_count):
    count = lax.axis_size("pulse")
    up = [(i, i + 1) for i in range(count - 1)]
    down = [(i + 1, i) for i in range(count - 1)]
    weights = resampling_weights(interp_tiles, tile_index, tile_count)
    tables = azimuth_tables()
    even = lax.axis_index("pulse") % 2 == 0
    ends = []
    first = 0
    for width in PARTS:
        columns = slice(first * LANES, (first + width) * LANES)
        tail = jnp.stack([phase_real[AZ - HALO :, columns], phase_imag[AZ - HALO :, columns]])
        head = jnp.stack([phase_real[:HALO, columns], phase_imag[:HALO, columns]])
        first += width
        if first < GROUPS:
            phase_real, phase_imag, tail, head = lax.optimization_barrier((phase_real, phase_imag, tail, head))
            ends.append((lax.ppermute(tail, "pulse", up), lax.ppermute(head, "pulse", down)))
            continue
        tail, head, *weights = lax.optimization_barrier((tail, head, *weights))
        away = {(a, c): ranks for a, b, c, ranks in RELAYS}
        ways = [
            [(32 * a + r, 32 * b + r) for a, b in pairs for r in range(32) if r not in away.get((a, b), ())]
            for pairs in (up, down)
        ]
        hops = [
            [(32 * legs[k] + r, 32 * legs[k + 1] + r) for *legs, ranks in RELAYS for r in ranks] for k in range(2)
        ]
        both = ("pulse", "range")
        top, bot = lax.ppermute(tail, both, ways[0]), lax.ppermute(head, both, ways[1])
        passed = lax.ppermute(jnp.where(even, head, tail), both, hops[0])
        passed = lax.ppermute(passed, both, hops[1])
        ends.append((jnp.where(even, top + passed, top), jnp.where(even, bot, bot + passed)))
    own = own_part(phase_real, phase_imag, weights)
    edges = [edge_weights(half) for half in weights]
    cells = []
    first = 0
    for width, (top, bot) in zip(PARTS, ends):
        sent = azimuth(first, width, own, top, bot, edges, tables)
        cells.append(lax.all_to_all(sent, "range", split_axis=0, concat_axis=0, tiled=True))
        first += width
    return tuple(range_transform(PARTS, cells, range_tables(PARTS)))


def solution(mesh):
    placed = (
        P("pulse", "range"),
        P("pulse", "range"),
        P("pulse", None, None, None),
        P("pulse", None),
        P("pulse"),
    )
    return jax.shard_map(
        shards,
        mesh=mesh,
        in_specs=placed,
        out_specs=(P(("pulse", "range"), None), P(("pulse", "range"), None)),
        check_vma=False,
    )
```

```python
import functools
import math

import jax
import jax.numpy as jnp
import ml_dtypes
import numpy as np
from jax import lax
from jax.experimental import pallas as pl
from jax.experimental.pallas import tpu as pltpu
from jax.sharding import PartitionSpec as P

S = 16384
AZ = 1024
BLOCK = 128
SLOTS = 5
HALO = 2 * BLOCK
LANES = 128
PARTS = (2, 2)
GROUPS = 4
ALL = tuple(range(32))
ONE_CORE = tuple(range(0, 32, 2))
MOST = tuple(r for r in range(32) if r % 2 == 0 or r // 8 == 1 + r // 2 % 2)
MIDDLE = tuple(r for r in ONE_CORE if r // 8 in (1, 2))
RELAYS = (
    (2, 0, 1, ALL),
    (5, 7, 6, ALL),
    (3, 5, 4, MOST),
    (4, 2, 3, MOST),
    (1, 3, 2, MIDDLE),
    (6, 4, 5, MIDDLE),
)
BF16 = jnp.bfloat16
F32 = jnp.float32


def unit_roots(numerators, length):
    angles = 2.0 * math.pi * (numerators % length) / length
    return np.cos(angles), -np.sin(angles)


def halves(table):
    high = table.astype(ml_dtypes.bfloat16)
    low = (table - high.astype(np.float64)).astype(ml_dtypes.bfloat16)
    return high, low


def azimuth_tables():
    idx = np.arange(256)
    real, imag = unit_roots(idx[:, None] * idx[None, :], 256)
    high, low = halves(np.concatenate([real, imag], axis=0) / 32.0)
    turns = []
    for a in range(1, 4):
        turn = np.stack(unit_roots(a * idx, 1024))
        turns.append(np.broadcast_to(turn[:, :, None], (2, 256, LANES)))
    return high, low, np.stack(turns).astype(np.float32)


def range_tables(parts):
    idx = np.arange(128)
    order = []
    first = 0
    for width in parts:
        for source in range(32):
            order += [4 * source + first + c for c in range(width)]
        first += width
    order = np.array(order)
    real, imag = unit_roots(idx[:, None] * order[None, :], 128)
    inner = np.block([[real, -imag], [imag, real]])
    turn = np.stack(unit_roots(idx[:, None] * idx[None, :], S)).astype(np.float32)
    real, imag = unit_roots(idx[:, None] * idx[None, :], 128)
    outer = np.block([[real, -imag], [imag, real]]) / 128.0
    return (*halves(inner), turn, *halves(outer))


def split(value):
    high = value.astype(BF16)
    return high, (value - high.astype(F32)).astype(BF16)


def dot(a, b, dims=(((1,), (0,)), ((), ()))):
    return lax.dot_general(a, b, dims, preferred_element_type=F32)


def own_kernel(re_ref, im_ref, wh_ref, wl_ref, out_ref, xh, xl):
    for i in range(AZ // BLOCK):
        rows = slice(i * BLOCK, (i + 1) * BLOCK)
        xh[rows], xl[rows] = split(jnp.concatenate([re_ref[rows], im_ref[rows]], axis=1))
    for b in range(AZ // BLOCK):
        low, high = max(b - 2, 0), min(b + 3, AZ // BLOCK)
        rows = slice(low * BLOCK, high * BLOCK)
        slots = slice((low - b + 2) * BLOCK, (high - b + 2) * BLOCK)
        wh, wl = wh_ref[b, :, slots], wl_ref[b, :, slots]
        out_ref[0, b * BLOCK : (b + 1) * BLOCK] = dot(wh, xh[rows]) + dot(wl, xh[rows]) + dot(wh, xl[rows])


def own_part(phase_real, phase_imag, weights):
    tile = pl.BlockSpec((8, BLOCK, SLOTS * BLOCK), lambda i: (0, 0, 0))
    return pl.pallas_call(
        own_kernel,
        grid=(GROUPS,),
        in_specs=[pl.BlockSpec((AZ, LANES), lambda i: (0, i))] * 2 + [tile, tile],
        out_specs=pl.BlockSpec((1, AZ, 2 * LANES), lambda i: (i, 0, 0)),
        out_shape=jax.ShapeDtypeStruct((GROUPS, AZ, 2 * LANES), F32),
        scratch_shapes=[pltpu.VMEM((AZ, 2 * LANES), BF16)] * 2,
        compiler_params=pltpu.CompilerParams(vmem_limit_bytes=40 * 1024 * 1024),
        cost_estimate=pl.CostEstimate(flops=1, bytes_accessed=1, transcendentals=0),
        name="own",
    )(phase_real, phase_imag, *weights)


def edge_weights(weights):
    none = jnp.zeros((BLOCK, BLOCK), weights.dtype)
    before = [weights[0, :, : 2 * BLOCK], jnp.concatenate([none, weights[1, :, :BLOCK]], axis=1)]
    after = [jnp.concatenate([weights[6, :, 4 * BLOCK :], none], axis=1), weights[7, :, 3 * BLOCK :]]
    return jnp.stack([jnp.concatenate(before, axis=0), jnp.concatenate(after, axis=0)])


def azimuth_kernel(own_ref, top_ref, bot_ref, wh_ref, wl_ref, dh_ref, dl_ref, tw_ref, out_ref, yh, yl):
    def put(row, cells):
        high, low = split(cells)
        for b in range(2):
            for a in range(4):
                rows = slice(b * BLOCK + a * 32, b * BLOCK + (a + 1) * 32)
                place = row // 4 + b * 32
                yh[a, place : place + 32] = high[rows]
                yl[a, place : place + 32] = low[rows]

    for side, (row, ref) in enumerate(((0, top_ref), (AZ - HALO, bot_ref))):
        high, low = split(jnp.concatenate([ref[0], ref[1]], axis=1))
        wh, wl = wh_ref[side], wl_ref[side]
        put(row, own_ref[0, row : row + HALO] + (dot(wh, high) + dot(wl, high) + dot(wh, low)))
    for row in range(HALO, AZ - HALO, HALO):
        put(row, own_ref[0, row : row + HALO])
    real, imag = [], []
    for a in range(4):
        four = dot(dh_ref[...], yh[a]) + dot(dl_ref[...], yh[a]) + dot(dh_ref[...], yl[a])
        vr = four[:256, :LANES] - four[256:, LANES:]
        vi = four[:256, LANES:] + four[256:, :LANES]
        if a:
            tr, ti = tw_ref[a - 1, 0], tw_ref[a - 1, 1]
            vr, vi = vr * tr - vi * ti, vr * ti + vi * tr
        real.append(vr)
        imag.append(vi)
    er, ei, fr, fi = real[0] + real[2], imag[0] + imag[2], real[0] - real[2], imag[0] - imag[2]
    gr, gi, hr, hi = real[1] + real[3], imag[1] + imag[3], real[1] - real[3], imag[1] - imag[3]
    bins = [(er + gr, ei + gi), (fr + hi, fi - hr), (er - gr, ei - gi), (fr - hi, fi + hr)]
    for quarter in range(4):
        for part in range(2):
            for t in range(8):
                out_ref[quarter * 8 + t, 0, part] = bins[quarter][part][t * 32 : (t + 1) * 32]


def azimuth(first, width, own, top, bot, weights, tables):
    fixed = lambda *shape: pl.BlockSpec(shape, lambda i: (0,) * len(shape))
    return pl.pallas_call(
        azimuth_kernel,
        grid=(width,),
        in_specs=[
            pl.BlockSpec((1, AZ, 2 * LANES), lambda i: (first + i, 0, 0)),
            pl.BlockSpec((2, HALO, LANES), lambda i: (0, 0, i)),
            pl.BlockSpec((2, HALO, LANES), lambda i: (0, 0, i)),
            fixed(2, HALO, HALO),
            fixed(2, HALO, HALO),
            fixed(512, 256),
            fixed(512, 256),
            fixed(3, 2, 256, LANES),
        ],
        out_specs=pl.BlockSpec((32, 1, 2, 32, LANES), lambda i: (0, i, 0, 0, 0)),
        out_shape=jax.ShapeDtypeStruct((32, width, 2, 32, LANES), F32),
        scratch_shapes=[pltpu.VMEM((4, 256, 2 * LANES), BF16)] * 2,
        compiler_params=pltpu.CompilerParams(vmem_limit_bytes=40 * 1024 * 1024),
        cost_estimate=pl.CostEstimate(
            flops=6 * width * 256 * AZ * 1152 * (100 if first else 1), bytes_accessed=width * 2**21, transcendentals=0
        ),
        name="azimuth",
    )(own, top, bot, *weights, *tables)


def range_kernel(parts, *refs):
    cells = refs[: len(parts)]
    ah_ref, al_ref, tw_ref, bh_ref, bl_ref, re_ref, im_ref = refs[len(parts) :]
    images = [ref.reshape(128 * 8, LANES) for ref in (re_ref, im_ref)]
    inner_table = jnp.concatenate([ah_ref[...], al_ref[...], ah_ref[...]], axis=1)
    outer_table = jnp.concatenate([bh_ref[...], bl_ref[...]], axis=0)
    flat = [ref.reshape(32 * width * 16, LANES) for ref, width in zip(cells, parts)]

    def rows_of(part, k):
        return jnp.concatenate(
            [ref[pl.ds(part * 8 + k, 32 * width, stride=16), :] for ref, width in zip(flat, parts)], axis=0
        )

    tr, ti = tw_ref[0], tw_ref[1]
    for pair in range(4):
        k0, k1 = 2 * pair, 2 * pair + 1
        full = jnp.concatenate(
            [jnp.concatenate([rows_of(part, k) for k in (k0, k1)], axis=1) for part in range(2)], axis=0
        )
        high, low = split(full)
        inner = dot(inner_table, jnp.concatenate([high, high, low], axis=0))
        turned = []
        for i in range(2):
            yr, yi = inner[:128, i * LANES : (i + 1) * LANES], inner[128:, i * LANES : (i + 1) * LANES]
            turned.append(jnp.concatenate([yr * tr - yi * ti, yr * ti + yi * tr], axis=1))
        high, low = split(jnp.concatenate(turned, axis=0))
        flip = (((1,), (1,)), ((), ()))
        wide = dot(outer_table, high, flip)
        outer = wide[:256] + wide[256:] + dot(bh_ref[...], low, flip)
        for i, k in enumerate((k0, k1)):
            for part in range(2):
                images[part][pl.ds(k, 128, stride=8), :] = outer[
                    part * 128 : (part + 1) * 128, i * LANES : (i + 1) * LANES
                ]


def range_transform(parts, cells, tables):
    fixed = lambda *shape: pl.BlockSpec(shape, lambda g: (0,) * len(shape))
    images = pl.pallas_call(
        functools.partial(range_kernel, parts),
        grid=(4,),
        in_specs=[pl.BlockSpec((32, width, 2, 8, LANES), lambda g: (0, 0, 0, g, 0)) for width in parts]
        + [fixed(256, 256), fixed(256, 256), fixed(2, 128, LANES), fixed(256, 256), fixed(256, 256)],
        out_specs=[pl.BlockSpec((1, 128, 8, LANES), lambda g: (g, 0, 0, 0))] * 2,
        out_shape=[jax.ShapeDtypeStruct((4, 128, 8, LANES), F32)] * 2,
        compiler_params=pltpu.CompilerParams(vmem_limit_bytes=40 * 1024 * 1024),
        cost_estimate=pl.CostEstimate(flops=4 * 32 * S * 256 * 3, bytes_accessed=8 * 2**20, transcendentals=0),
        name="range",
    )(*cells, *tables)
    return [image.transpose(0, 2, 1, 3).reshape(32, S) for image in images]


def ends_kernel(real_tail, imag_tail, real_head, imag_head, tail_ref, head_ref):
    for out_ref, parts in ((tail_ref, (real_tail, imag_tail)), (head_ref, (real_head, imag_head))):
        for part, ref in enumerate(parts):
            out_ref[part] = ref[...]


def block_ends(chunk, phase_real, phase_imag):
    block = lambda rows: pl.BlockSpec((HALO, 2 * LANES), lambda i: (rows, chunk))
    return pl.pallas_call(
        ends_kernel,
        grid=(1,),
        in_specs=[block(AZ // HALO - 1)] * 2 + [block(0)] * 2,
        out_specs=[pl.BlockSpec((2, HALO, 2 * LANES), lambda i: (0, 0, 0))] * 2,
        out_shape=[jax.ShapeDtypeStruct((2, HALO, 2 * LANES), F32)] * 2,
        compiler_params=pltpu.CompilerParams(vmem_limit_bytes=60 * 1024 * 1024),
        cost_estimate=pl.CostEstimate(flops=0, bytes_accessed=2 * 2**20, transcendentals=0),
        name="ends",
    )(phase_real, phase_imag, phase_real, phase_imag)


def resampling_weights(interp_tiles, tile_index, tile_count):
    tiles_dev = interp_tiles.shape[0]
    first_block = lax.axis_index("pulse") * tiles_dev
    offsets = tile_index - (first_block + jnp.arange(tiles_dev, dtype=jnp.int32))[:, None]
    live = jnp.arange(SLOTS, dtype=jnp.int32)[None, :] < tile_count[:, None]
    places = jnp.arange(-2, 3, dtype=jnp.int32)
    chosen = ((offsets[:, None, :] == places[None, :, None]) & live[:, None, :]).astype(F32)
    weights = jnp.sum(interp_tiles[:, None] * chosen[:, :, :, None, None], axis=2)
    weights = weights.reshape(tiles_dev, SLOTS, 32, 4, BLOCK).transpose(0, 3, 2, 1, 4)
    weights = weights.reshape(tiles_dev, BLOCK, SLOTS * BLOCK)
    high = lax.reduce_precision(weights, 8, 7)
    return high.astype(BF16), (weights - high).astype(BF16)


def shards(phase_real, phase_imag, interp_tiles, tile_index, tile_count):
    count = lax.axis_size("pulse")
    up = [(i, i + 1) for i in range(count - 1)]
    down = [(i + 1, i) for i in range(count - 1)]
    weights = resampling_weights(interp_tiles, tile_index, tile_count)
    tables = azimuth_tables()
    even = lax.axis_index("pulse") % 2 == 0
    ends = []
    first = 0
    for width in PARTS:
        tail, head = block_ends(first // width, phase_real, phase_imag)
        first += width
        if first < GROUPS:
            phase_real, phase_imag, tail, head = lax.optimization_barrier((phase_real, phase_imag, tail, head))
            ends.append((lax.ppermute(tail, "pulse", up), lax.ppermute(head, "pulse", down)))
            continue
        away = {(a, c): ranks for a, b, c, ranks in RELAYS}
        ways = [
            [(32 * a + r, 32 * b + r) for a, b in pairs for r in range(32) if r not in away.get((a, b), ())]
            for pairs in (up, down)
        ]
        hops = [
            [(32 * legs[k] + r, 32 * legs[k + 1] + r) for *legs, ranks in RELAYS for r in ranks] for k in range(2)
        ]
        both = ("pulse", "range")
        passed = lax.ppermute(jnp.where(even, head, tail), both, hops[0])
        tail, head, *weights = lax.optimization_barrier((tail, head, *weights))
        top, bot = lax.ppermute(tail, both, ways[0]), lax.ppermute(head, both, ways[1])
        passed = lax.ppermute(passed, both, hops[1])
        ends.append((jnp.where(even, top + passed, top), jnp.where(even, bot, bot + passed)))
    own = own_part(phase_real, phase_imag, weights)
    edges = [edge_weights(half) for half in weights]
    cells = []
    first = 0
    for width, (top, bot) in zip(PARTS, ends):
        sent = azimuth(first, width, own, top, bot, edges, tables)
        cells.append(lax.all_to_all(sent, "range", split_axis=0, concat_axis=0, tiled=True))
        first += width
    return tuple(range_transform(PARTS, cells, range_tables(PARTS)))


def solution(mesh):
    placed = (
        P("pulse", "range"),
        P("pulse", "range"),
        P("pulse", None, None, None),
        P("pulse", None),
        P("pulse"),
    )
    return jax.shard_map(
        shards,
        mesh=mesh,
        in_specs=placed,
        out_specs=(P(("pulse", "range"), None), P(("pulse", "range"), None)),
        check_vma=False,
    )
```

```python
import functools
import math

import jax
import jax.numpy as jnp
import ml_dtypes
import numpy as np
from jax import lax
from jax.experimental import pallas as pl
from jax.experimental.pallas import tpu as pltpu
from jax.sharding import PartitionSpec as P

S = 16384
AZ = 1024
BLOCK = 128
SLOTS = 5
HALO = 2 * BLOCK
LANES = 128
PARTS = (2, 2)
GROUPS = 4
ALL = tuple(range(32))
ONE_CORE = tuple(range(0, 32, 2))
MOST = tuple(r for r in range(32) if r % 2 == 0 or r // 8 == 1 + r // 2 % 2)
MIDDLE = tuple(r for r in ONE_CORE if r // 8 in (1, 2))
RELAYS = (
    (2, 0, 1, ALL),
    (5, 7, 6, ALL),
    (3, 5, 4, MOST),
    (4, 2, 3, MOST),
    (1, 3, 2, MIDDLE),
    (6, 4, 5, MIDDLE),
)
BF16 = jnp.bfloat16
F32 = jnp.float32


def unit_roots(numerators, length):
    angles = 2.0 * math.pi * (numerators % length) / length
    return np.cos(angles), -np.sin(angles)


def halves(table):
    high = table.astype(ml_dtypes.bfloat16)
    low = (table - high.astype(np.float64)).astype(ml_dtypes.bfloat16)
    return high, low


def azimuth_tables():
    idx = np.arange(256)
    real, imag = unit_roots(idx[:, None] * idx[None, :], 256)
    high, low = halves(np.concatenate([real, imag], axis=0) / 32.0)
    turns = []
    for a in range(1, 4):
        turn = np.stack(unit_roots(a * idx, 1024))
        turns.append(np.broadcast_to(turn[:, :, None], (2, 256, LANES)))
    return high, low, np.stack(turns).astype(np.float32)


def range_tables(parts):
    idx = np.arange(128)
    order = []
    first = 0
    for width in parts:
        for source in range(32):
            order += [4 * source + first + c for c in range(width)]
        first += width
    order = np.array(order)
    real, imag = unit_roots(idx[:, None] * order[None, :], 128)
    inner = np.block([[real, -imag], [imag, real]])
    turn = np.stack(unit_roots(idx[:, None] * idx[None, :], S)).astype(np.float32)
    real, imag = unit_roots(idx[:, None] * idx[None, :], 128)
    outer = np.block([[real, -imag], [imag, real]]) / 128.0
    return (*halves(inner), turn, *halves(outer))


def split(value):
    high = value.astype(BF16)
    return high, (value - high.astype(F32)).astype(BF16)


def dot(a, b, dims=(((1,), (0,)), ((), ()))):
    return lax.dot_general(a, b, dims, preferred_element_type=F32)


def own_kernel(re_ref, im_ref, wh_ref, wl_ref, out_ref, xh, xl):
    for i in range(AZ // BLOCK):
        rows = slice(i * BLOCK, (i + 1) * BLOCK)
        xh[rows], xl[rows] = split(jnp.concatenate([re_ref[rows], im_ref[rows]], axis=1))
    for b in range(AZ // BLOCK):
        low, high = max(b - 2, 0), min(b + 3, AZ // BLOCK)
        rows = slice(low * BLOCK, high * BLOCK)
        slots = slice((low - b + 2) * BLOCK, (high - b + 2) * BLOCK)
        wh, wl = wh_ref[b, :, slots], wl_ref[b, :, slots]
        out_ref[0, b * BLOCK : (b + 1) * BLOCK] = dot(wh, xh[rows]) + dot(wl, xh[rows]) + dot(wh, xl[rows])


def own_part(phase_real, phase_imag, weights):
    tile = pl.BlockSpec((8, BLOCK, SLOTS * BLOCK), lambda i: (0, 0, 0))
    return pl.pallas_call(
        own_kernel,
        grid=(GROUPS,),
        in_specs=[pl.BlockSpec((AZ, LANES), lambda i: (0, i))] * 2 + [tile, tile],
        out_specs=pl.BlockSpec((1, AZ, 2 * LANES), lambda i: (i, 0, 0)),
        out_shape=jax.ShapeDtypeStruct((GROUPS, AZ, 2 * LANES), F32),
        scratch_shapes=[pltpu.VMEM((AZ, 2 * LANES), BF16)] * 2,
        compiler_params=pltpu.CompilerParams(vmem_limit_bytes=40 * 1024 * 1024),
        cost_estimate=pl.CostEstimate(flops=1, bytes_accessed=1, transcendentals=0),
        name="own",
    )(phase_real, phase_imag, *weights)


def edge_weights(weights):
    none = jnp.zeros((BLOCK, BLOCK), weights.dtype)
    before = [weights[0, :, : 2 * BLOCK], jnp.concatenate([none, weights[1, :, :BLOCK]], axis=1)]
    after = [jnp.concatenate([weights[6, :, 4 * BLOCK :], none], axis=1), weights[7, :, 3 * BLOCK :]]
    return jnp.stack([jnp.concatenate(before, axis=0), jnp.concatenate(after, axis=0)])


def azimuth_kernel(own_ref, top_ref, bot_ref, wh_ref, wl_ref, dh_ref, dl_ref, tw_ref, out_ref, yh, yl):
    def put(row, cells):
        high, low = split(cells)
        for b in range(2):
            for a in range(4):
                rows = slice(b * BLOCK + a * 32, b * BLOCK + (a + 1) * 32)
                place = row // 4 + b * 32
                yh[a, place : place + 32] = high[rows]
                yl[a, place : place + 32] = low[rows]

    for side, (row, ref) in enumerate(((0, top_ref), (AZ - HALO, bot_ref))):
        high, low = split(jnp.concatenate([ref[0], ref[1]], axis=1))
        wh, wl = wh_ref[side], wl_ref[side]
        put(row, own_ref[0, row : row + HALO] + (dot(wh, high) + dot(wl, high) + dot(wh, low)))
    for row in range(HALO, AZ - HALO, HALO):
        put(row, own_ref[0, row : row + HALO])
    real, imag = [], []
    for a in range(4):
        four = dot(dh_ref[...], yh[a]) + dot(dl_ref[...], yh[a]) + dot(dh_ref[...], yl[a])
        vr = four[:256, :LANES] - four[256:, LANES:]
        vi = four[:256, LANES:] + four[256:, :LANES]
        if a:
            tr, ti = tw_ref[a - 1, 0], tw_ref[a - 1, 1]
            vr, vi = vr * tr - vi * ti, vr * ti + vi * tr
        real.append(vr)
        imag.append(vi)
    er, ei, fr, fi = real[0] + real[2], imag[0] + imag[2], real[0] - real[2], imag[0] - imag[2]
    gr, gi, hr, hi = real[1] + real[3], imag[1] + imag[3], real[1] - real[3], imag[1] - imag[3]
    bins = [(er + gr, ei + gi), (fr + hi, fi - hr), (er - gr, ei - gi), (fr - hi, fi + hr)]
    for quarter in range(4):
        for part in range(2):
            for t in range(8):
                out_ref[quarter * 8 + t, 0, part] = bins[quarter][part][t * 32 : (t + 1) * 32]


def azimuth(first, width, own, top, bot, weights, tables):
    fixed = lambda *shape: pl.BlockSpec(shape, lambda i: (0,) * len(shape))
    return pl.pallas_call(
        azimuth_kernel,
        grid=(width,),
        in_specs=[
            pl.BlockSpec((1, AZ, 2 * LANES), lambda i: (first + i, 0, 0)),
            pl.BlockSpec((2, HALO, LANES), lambda i: (0, 0, i)),
            pl.BlockSpec((2, HALO, LANES), lambda i: (0, 0, i)),
            fixed(2, HALO, HALO),
            fixed(2, HALO, HALO),
            fixed(512, 256),
            fixed(512, 256),
            fixed(3, 2, 256, LANES),
        ],
        out_specs=pl.BlockSpec((32, 1, 2, 32, LANES), lambda i: (0, i, 0, 0, 0)),
        out_shape=jax.ShapeDtypeStruct((32, width, 2, 32, LANES), F32),
        scratch_shapes=[pltpu.VMEM((4, 256, 2 * LANES), BF16)] * 2,
        compiler_params=pltpu.CompilerParams(vmem_limit_bytes=40 * 1024 * 1024),
        cost_estimate=pl.CostEstimate(
            flops=6 * width * 256 * AZ * 1152 * (100 if first else 1), bytes_accessed=width * 2**21, transcendentals=0
        ),
        name="azimuth",
    )(own, top, bot, *weights, *tables)


def range_kernel(parts, *refs):
    cells = refs[: len(parts)]
    ah_ref, al_ref, tw_ref, bh_ref, bl_ref, re_ref, im_ref = refs[len(parts) :]
    images = [ref.reshape(128 * 8, LANES) for ref in (re_ref, im_ref)]
    inner_table = jnp.concatenate([ah_ref[...], al_ref[...], ah_ref[...]], axis=1)
    outer_table = jnp.concatenate([bh_ref[...], bl_ref[...]], axis=0)
    flat = [ref.reshape(32 * width * 16, LANES) for ref, width in zip(cells, parts)]

    def rows_of(part, k):
        return jnp.concatenate(
            [ref[pl.ds(part * 8 + k, 32 * width, stride=16), :] for ref, width in zip(flat, parts)], axis=0
        )

    tr, ti = tw_ref[0], tw_ref[1]
    for pair in range(4):
        k0, k1 = 2 * pair, 2 * pair + 1
        full = jnp.concatenate(
            [jnp.concatenate([rows_of(part, k) for k in (k0, k1)], axis=1) for part in range(2)], axis=0
        )
        high, low = split(full)
        inner = dot(inner_table, jnp.concatenate([high, high, low], axis=0))
        turned = []
        for i in range(2):
            yr, yi = inner[:128, i * LANES : (i + 1) * LANES], inner[128:, i * LANES : (i + 1) * LANES]
            turned.append(jnp.concatenate([yr * tr - yi * ti, yr * ti + yi * tr], axis=1))
        high, low = split(jnp.concatenate(turned, axis=0))
        flip = (((1,), (1,)), ((), ()))
        wide = dot(outer_table, high, flip)
        outer = wide[:256] + wide[256:] + dot(bh_ref[...], low, flip)
        for i, k in enumerate((k0, k1)):
            for part in range(2):
                images[part][pl.ds(k, 128, stride=8), :] = outer[
                    part * 128 : (part + 1) * 128, i * LANES : (i + 1) * LANES
                ]


def range_transform(parts, cells, tables):
    fixed = lambda *shape: pl.BlockSpec(shape, lambda g: (0,) * len(shape))
    images = pl.pallas_call(
        functools.partial(range_kernel, parts),
        grid=(4,),
        in_specs=[pl.BlockSpec((32, width, 2, 8, LANES), lambda g: (0, 0, 0, g, 0)) for width in parts]
        + [fixed(256, 256), fixed(256, 256), fixed(2, 128, LANES), fixed(256, 256), fixed(256, 256)],
        out_specs=[pl.BlockSpec((1, 128, 8, LANES), lambda g: (g, 0, 0, 0))] * 2,
        out_shape=[jax.ShapeDtypeStruct((4, 128, 8, LANES), F32)] * 2,
        compiler_params=pltpu.CompilerParams(vmem_limit_bytes=40 * 1024 * 1024),
        cost_estimate=pl.CostEstimate(flops=4 * 32 * S * 256 * 3, bytes_accessed=8 * 2**20, transcendentals=0),
        name="range",
    )(*cells, *tables)
    return [image.transpose(0, 2, 1, 3).reshape(32, S) for image in images]


def ends_kernel(real_tail, imag_tail, real_head, imag_head, tail_ref, head_ref):
    for out_ref, parts in ((tail_ref, (real_tail, imag_tail)), (head_ref, (real_head, imag_head))):
        for part, ref in enumerate(parts):
            out_ref[part] = ref[...]


def block_ends(chunk, phase_real, phase_imag):
    block = lambda rows: pl.BlockSpec((HALO, 2 * LANES), lambda i: (rows, chunk))
    return pl.pallas_call(
        ends_kernel,
        grid=(1,),
        in_specs=[block(AZ // HALO - 1)] * 2 + [block(0)] * 2,
        out_specs=[pl.BlockSpec((2, HALO, 2 * LANES), lambda i: (0, 0, 0))] * 2,
        out_shape=[jax.ShapeDtypeStruct((2, HALO, 2 * LANES), F32)] * 2,
        compiler_params=pltpu.CompilerParams(vmem_limit_bytes=60 * 1024 * 1024),
        cost_estimate=pl.CostEstimate(flops=0, bytes_accessed=2 * 2**20, transcendentals=0),
        name="ends",
    )(phase_real, phase_imag, phase_real, phase_imag)


def resampling_weights(interp_tiles, tile_index, tile_count):
    tiles_dev = interp_tiles.shape[0]
    first_block = lax.axis_index("pulse") * tiles_dev
    offsets = tile_index - (first_block + jnp.arange(tiles_dev, dtype=jnp.int32))[:, None]
    live = jnp.arange(SLOTS, dtype=jnp.int32)[None, :] < tile_count[:, None]
    places = jnp.arange(-2, 3, dtype=jnp.int32)
    chosen = ((offsets[:, None, :] == places[None, :, None]) & live[:, None, :]).astype(F32)
    weights = jnp.sum(interp_tiles[:, None] * chosen[:, :, :, None, None], axis=2)
    weights = weights.reshape(tiles_dev, SLOTS, 32, 4, BLOCK).transpose(0, 3, 2, 1, 4)
    weights = weights.reshape(tiles_dev, BLOCK, SLOTS * BLOCK)
    high = lax.reduce_precision(weights, 8, 7)
    return high.astype(BF16), (weights - high).astype(BF16)


def shards(phase_real, phase_imag, interp_tiles, tile_index, tile_count):
    count = lax.axis_size("pulse")
    up = [(i, i + 1) for i in range(count - 1)]
    down = [(i + 1, i) for i in range(count - 1)]
    weights = resampling_weights(interp_tiles, tile_index, tile_count)
    tables = azimuth_tables()
    even = lax.axis_index("pulse") % 2 == 0
    ends = []
    first = 0
    for width in PARTS:
        tail, head = block_ends(first // width, phase_real, phase_imag)
        first += width
        if first < GROUPS:
            phase_real, phase_imag, tail, head = lax.optimization_barrier((phase_real, phase_imag, tail, head))
            ends.append((lax.ppermute(tail, "pulse", up), lax.ppermute(head, "pulse", down)))
            continue
        away = {(a, c): ranks for a, b, c, ranks in RELAYS}
        ways = [
            [(32 * a + r, 32 * b + r) for a, b in pairs for r in range(32) if r not in away.get((a, b), ())]
            for pairs in (up, down)
        ]
        hops = [
            [(32 * legs[k] + r, 32 * legs[k + 1] + r) for *legs, ranks in RELAYS for r in ranks] for k in range(2)
        ]
        both = ("pulse", "range")
        passed = lax.ppermute(jnp.where(even, head, tail), both, hops[0])
        own = own_part(phase_real, phase_imag, weights)
        edges = [edge_weights(half) for half in weights]
        tail, head, own, *edges = lax.optimization_barrier((tail, head, own, *edges))
        top, bot = lax.ppermute(tail, both, ways[0]), lax.ppermute(head, both, ways[1])
        passed = lax.ppermute(passed, both, hops[1])
        ends.append((jnp.where(even, top + passed, top), jnp.where(even, bot, bot + passed)))
    cells = []
    first = 0
    for width, (top, bot) in zip(PARTS, ends):
        sent = azimuth(first, width, own, top, bot, edges, tables)
        cells.append(lax.all_to_all(sent, "range", split_axis=0, concat_axis=0, tiled=True))
        first += width
    return tuple(range_transform(PARTS, cells, range_tables(PARTS)))


def solution(mesh):
    placed = (
        P("pulse", "range"),
        P("pulse", "range"),
        P("pulse", None, None, None),
        P("pulse", None),
        P("pulse"),
    )
    return jax.shard_map(
        shards,
        mesh=mesh,
        in_specs=placed,
        out_specs=(P(("pulse", "range"), None), P(("pulse", "range"), None)),
        check_vma=False,
    )
```

```python
import functools
import math

import jax
import jax.numpy as jnp
import ml_dtypes
import numpy as np
from jax import lax
from jax.experimental import pallas as pl
from jax.experimental.pallas import tpu as pltpu
from jax.sharding import PartitionSpec as P

S = 16384
AZ = 1024
BLOCK = 128
SLOTS = 5
HALO = 2 * BLOCK
LANES = 128
PARTS = (2, 2)
GROUPS = 4
ALL = tuple(range(32))
ONE_CORE = tuple(range(0, 32, 2))
MOST = tuple(r for r in range(32) if r % 2 == 0 or r // 8 == 1 + r // 2 % 2)
MIDDLE = tuple(r for r in ONE_CORE if r // 8 in (1, 2))
RELAYS = (
    (2, 0, 1, ALL),
    (5, 7, 6, ALL),
    (3, 5, 4, MOST),
    (4, 2, 3, MOST),
    (1, 3, 2, MIDDLE),
    (6, 4, 5, MIDDLE),
)
BF16 = jnp.bfloat16
F32 = jnp.float32


def unit_roots(numerators, length):
    angles = 2.0 * math.pi * (numerators % length) / length
    return np.cos(angles), -np.sin(angles)


def halves(table):
    high = table.astype(ml_dtypes.bfloat16)
    low = (table - high.astype(np.float64)).astype(ml_dtypes.bfloat16)
    return high, low


def azimuth_tables():
    idx = np.arange(256)
    real, imag = unit_roots(idx[:, None] * idx[None, :], 256)
    high, low = halves(np.concatenate([real, imag], axis=0) / 32.0)
    turns = []
    for a in range(1, 4):
        turn = np.stack(unit_roots(a * idx, 1024))
        turns.append(np.broadcast_to(turn[:, :, None], (2, 256, LANES)))
    return high, low, np.stack(turns).astype(np.float32)


def range_tables(parts):
    idx = np.arange(128)
    order = []
    first = 0
    for width in parts:
        for source in range(32):
            order += [4 * source + first + c for c in range(width)]
        first += width
    order = np.array(order)
    real, imag = unit_roots(idx[:, None] * order[None, :], 128)
    inner = np.block([[real, -imag], [imag, real]])
    turn = np.stack(unit_roots(idx[:, None] * idx[None, :], S)).astype(np.float32)
    real, imag = unit_roots(idx[:, None] * idx[None, :], 128)
    outer = np.block([[real, -imag], [imag, real]]) / 128.0
    return (*halves(inner), turn, *halves(outer))


def split(value):
    high = value.astype(BF16)
    return high, (value - high.astype(F32)).astype(BF16)


def dot(a, b, dims=(((1,), (0,)), ((), ()))):
    return lax.dot_general(a, b, dims, preferred_element_type=F32)


def own_kernel(re_ref, im_ref, wh_ref, wl_ref, out_ref, xh, xl):
    for i in range(AZ // BLOCK):
        rows = slice(i * BLOCK, (i + 1) * BLOCK)
        xh[rows], xl[rows] = split(jnp.concatenate([re_ref[rows], im_ref[rows]], axis=1))
    for b in range(AZ // BLOCK):
        low, high = max(b - 2, 0), min(b + 3, AZ // BLOCK)
        rows = slice(low * BLOCK, high * BLOCK)
        slots = slice((low - b + 2) * BLOCK, (high - b + 2) * BLOCK)
        wh, wl = wh_ref[b, :, slots], wl_ref[b, :, slots]
        out_ref[0, b * BLOCK : (b + 1) * BLOCK] = dot(wh, xh[rows]) + dot(wl, xh[rows]) + dot(wh, xl[rows])


def own_part(phase_real, phase_imag, weights):
    tile = pl.BlockSpec((8, BLOCK, SLOTS * BLOCK), lambda i: (0, 0, 0))
    return pl.pallas_call(
        own_kernel,
        grid=(GROUPS,),
        in_specs=[pl.BlockSpec((AZ, LANES), lambda i: (0, i))] * 2 + [tile, tile],
        out_specs=pl.BlockSpec((1, AZ, 2 * LANES), lambda i: (i, 0, 0)),
        out_shape=jax.ShapeDtypeStruct((GROUPS, AZ, 2 * LANES), F32),
        scratch_shapes=[pltpu.VMEM((AZ, 2 * LANES), BF16)] * 2,
        compiler_params=pltpu.CompilerParams(vmem_limit_bytes=40 * 1024 * 1024),
        cost_estimate=pl.CostEstimate(flops=1, bytes_accessed=1, transcendentals=0),
        name="own",
    )(phase_real, phase_imag, *weights)


def edge_weights(weights):
    none = jnp.zeros((BLOCK, BLOCK), weights.dtype)
    before = [weights[0, :, : 2 * BLOCK], jnp.concatenate([none, weights[1, :, :BLOCK]], axis=1)]
    after = [jnp.concatenate([weights[6, :, 4 * BLOCK :], none], axis=1), weights[7, :, 3 * BLOCK :]]
    return jnp.stack([jnp.concatenate(before, axis=0), jnp.concatenate(after, axis=0)])


def azimuth_kernel(own_ref, top_ref, bot_ref, wh_ref, wl_ref, dh_ref, dl_ref, tw_ref, out_ref, yh, yl):
    def put(row, cells):
        high, low = split(cells)
        for b in range(2):
            for a in range(4):
                rows = slice(b * BLOCK + a * 32, b * BLOCK + (a + 1) * 32)
                place = row // 4 + b * 32
                yh[a, place : place + 32] = high[rows]
                yl[a, place : place + 32] = low[rows]

    for side, (row, ref) in enumerate(((0, top_ref), (AZ - HALO, bot_ref))):
        high, low = split(jnp.concatenate([ref[0], ref[1]], axis=1))
        wh, wl = wh_ref[side], wl_ref[side]
        put(row, own_ref[0, row : row + HALO] + (dot(wh, high) + dot(wl, high) + dot(wh, low)))
    for row in range(HALO, AZ - HALO, HALO):
        put(row, own_ref[0, row : row + HALO])
    real, imag = [], []
    for a in range(4):
        four = dot(dh_ref[...], yh[a]) + dot(dl_ref[...], yh[a]) + dot(dh_ref[...], yl[a])
        vr = four[:256, :LANES] - four[256:, LANES:]
        vi = four[:256, LANES:] + four[256:, :LANES]
        if a:
            tr, ti = tw_ref[a - 1, 0], tw_ref[a - 1, 1]
            vr, vi = vr * tr - vi * ti, vr * ti + vi * tr
        real.append(vr)
        imag.append(vi)
    er, ei, fr, fi = real[0] + real[2], imag[0] + imag[2], real[0] - real[2], imag[0] - imag[2]
    gr, gi, hr, hi = real[1] + real[3], imag[1] + imag[3], real[1] - real[3], imag[1] - imag[3]
    bins = [(er + gr, ei + gi), (fr + hi, fi - hr), (er - gr, ei - gi), (fr - hi, fi + hr)]
    for quarter in range(4):
        for part in range(2):
            for t in range(8):
                out_ref[quarter * 8 + t, 0, part] = bins[quarter][part][t * 32 : (t + 1) * 32]


def azimuth(first, width, own, top, bot, weights, tables):
    fixed = lambda *shape: pl.BlockSpec(shape, lambda i: (0,) * len(shape))
    return pl.pallas_call(
        azimuth_kernel,
        grid=(width,),
        in_specs=[
            pl.BlockSpec((1, AZ, 2 * LANES), lambda i: (first + i, 0, 0)),
            pl.BlockSpec((2, HALO, LANES), lambda i: (0, 0, i)),
            pl.BlockSpec((2, HALO, LANES), lambda i: (0, 0, i)),
            fixed(2, HALO, HALO),
            fixed(2, HALO, HALO),
            fixed(512, 256),
            fixed(512, 256),
            fixed(3, 2, 256, LANES),
        ],
        out_specs=pl.BlockSpec((32, 1, 2, 32, LANES), lambda i: (0, i, 0, 0, 0)),
        out_shape=jax.ShapeDtypeStruct((32, width, 2, 32, LANES), F32),
        scratch_shapes=[pltpu.VMEM((4, 256, 2 * LANES), BF16)] * 2,
        compiler_params=pltpu.CompilerParams(vmem_limit_bytes=60 * 1024 * 1024),
        cost_estimate=pl.CostEstimate(
            flops=6 * width * 256 * AZ * 1152 * (100 if first else 1), bytes_accessed=width * 2**21, transcendentals=0
        ),
        name="azimuth",
    )(own, top, bot, *weights, *tables)


def range_kernel(parts, *refs):
    cells = refs[: len(parts)]
    ah_ref, al_ref, tw_ref, bh_ref, bl_ref, re_ref, im_ref = refs[len(parts) :]
    images = [ref.reshape(128 * 8, LANES) for ref in (re_ref, im_ref)]
    inner_table = jnp.concatenate([ah_ref[...], al_ref[...], ah_ref[...]], axis=1)
    outer_table = jnp.concatenate([bh_ref[...], bl_ref[...]], axis=0)
    flat = [ref.reshape(32 * width * 16, LANES) for ref, width in zip(cells, parts)]

    def rows_of(part, k):
        return jnp.concatenate(
            [ref[pl.ds(part * 8 + k, 32 * width, stride=16), :] for ref, width in zip(flat, parts)], axis=0
        )

    tr, ti = tw_ref[0], tw_ref[1]
    for pair in range(4):
        k0, k1 = 2 * pair, 2 * pair + 1
        full = jnp.concatenate(
            [jnp.concatenate([rows_of(part, k) for k in (k0, k1)], axis=1) for part in range(2)], axis=0
        )
        high, low = split(full)
        inner = dot(inner_table, jnp.concatenate([high, high, low], axis=0))
        turned = []
        for i in range(2):
            yr, yi = inner[:128, i * LANES : (i + 1) * LANES], inner[128:, i * LANES : (i + 1) * LANES]
            turned.append(jnp.concatenate([yr * tr - yi * ti, yr * ti + yi * tr], axis=1))
        high, low = split(jnp.concatenate(turned, axis=0))
        flip = (((1,), (1,)), ((), ()))
        wide = dot(outer_table, high, flip)
        outer = wide[:256] + wide[256:] + dot(bh_ref[...], low, flip)
        for i, k in enumerate((k0, k1)):
            for part in range(2):
                images[part][pl.ds(k, 128, stride=8), :] = outer[
                    part * 128 : (part + 1) * 128, i * LANES : (i + 1) * LANES
                ]


def range_transform(parts, cells, tables):
    fixed = lambda *shape: pl.BlockSpec(shape, lambda g: (0,) * len(shape))
    images = pl.pallas_call(
        functools.partial(range_kernel, parts),
        grid=(4,),
        in_specs=[pl.BlockSpec((32, width, 2, 8, LANES), lambda g: (0, 0, 0, g, 0)) for width in parts]
        + [fixed(256, 256), fixed(256, 256), fixed(2, 128, LANES), fixed(256, 256), fixed(256, 256)],
        out_specs=[pl.BlockSpec((1, 128, 8, LANES), lambda g: (g, 0, 0, 0))] * 2,
        out_shape=[jax.ShapeDtypeStruct((4, 128, 8, LANES), F32)] * 2,
        compiler_params=pltpu.CompilerParams(vmem_limit_bytes=40 * 1024 * 1024),
        cost_estimate=pl.CostEstimate(flops=4 * 32 * S * 256 * 3, bytes_accessed=8 * 2**20, transcendentals=0),
        name="range",
    )(*cells, *tables)
    return [image.transpose(0, 2, 1, 3).reshape(32, S) for image in images]


def ends_kernel(real_tail, imag_tail, real_head, imag_head, tail_ref, head_ref):
    for out_ref, parts in ((tail_ref, (real_tail, imag_tail)), (head_ref, (real_head, imag_head))):
        for part, ref in enumerate(parts):
            out_ref[part] = ref[...]


def block_ends(chunk, phase_real, phase_imag):
    block = lambda rows: pl.BlockSpec((HALO, 2 * LANES), lambda i: (rows, chunk))
    return pl.pallas_call(
        ends_kernel,
        grid=(1,),
        in_specs=[block(AZ // HALO - 1)] * 2 + [block(0)] * 2,
        out_specs=[pl.BlockSpec((2, HALO, 2 * LANES), lambda i: (0, 0, 0))] * 2,
        out_shape=[jax.ShapeDtypeStruct((2, HALO, 2 * LANES), F32)] * 2,
        compiler_params=pltpu.CompilerParams(vmem_limit_bytes=60 * 1024 * 1024),
        cost_estimate=pl.CostEstimate(flops=0, bytes_accessed=2 * 2**20, transcendentals=0),
        name="ends",
    )(phase_real, phase_imag, phase_real, phase_imag)


def resampling_weights(interp_tiles, tile_index, tile_count):
    tiles_dev = interp_tiles.shape[0]
    first_block = lax.axis_index("pulse") * tiles_dev
    offsets = tile_index - (first_block + jnp.arange(tiles_dev, dtype=jnp.int32))[:, None]
    live = jnp.arange(SLOTS, dtype=jnp.int32)[None, :] < tile_count[:, None]
    places = jnp.arange(-2, 3, dtype=jnp.int32)
    chosen = ((offsets[:, None, :] == places[None, :, None]) & live[:, None, :]).astype(F32)
    weights = jnp.sum(interp_tiles[:, None] * chosen[:, :, :, None, None], axis=2)
    weights = weights.reshape(tiles_dev, SLOTS, 32, 4, BLOCK).transpose(0, 3, 2, 1, 4)
    weights = weights.reshape(tiles_dev, BLOCK, SLOTS * BLOCK)
    high = lax.reduce_precision(weights, 8, 7)
    return high.astype(BF16), (weights - high).astype(BF16)


def shards(phase_real, phase_imag, interp_tiles, tile_index, tile_count):
    count = lax.axis_size("pulse")
    up = [(i, i + 1) for i in range(count - 1)]
    down = [(i + 1, i) for i in range(count - 1)]
    weights = resampling_weights(interp_tiles, tile_index, tile_count)
    tables = azimuth_tables()
    even = lax.axis_index("pulse") % 2 == 0
    ends = []
    first = 0
    for width in PARTS:
        tail, head = block_ends(first // width, phase_real, phase_imag)
        first += width
        if first < GROUPS:
            phase_real, phase_imag, tail, head = lax.optimization_barrier((phase_real, phase_imag, tail, head))
            ends.append((lax.ppermute(tail, "pulse", up), lax.ppermute(head, "pulse", down)))
            continue
        away = {(a, c): ranks for a, b, c, ranks in RELAYS}
        ways = [
            [(32 * a + r, 32 * b + r) for a, b in pairs for r in range(32) if r not in away.get((a, b), ())]
            for pairs in (up, down)
        ]
        hops = [
            [(32 * legs[k] + r, 32 * legs[k + 1] + r) for *legs, ranks in RELAYS for r in ranks] for k in range(2)
        ]
        both = ("pulse", "range")
        passed = lax.ppermute(jnp.where(even, head, tail), both, hops[0])
        tail, head, *weights = lax.optimization_barrier((tail, head, *weights))
        top, bot = lax.ppermute(tail, both, ways[0]), lax.ppermute(head, both, ways[1])
        passed = lax.ppermute(passed, both, hops[1])
        ends.append((jnp.where(even, top + passed, top), jnp.where(even, bot, bot + passed)))
    own = own_part(phase_real, phase_imag, weights)
    edges = [edge_weights(half) for half in weights]
    cells = []
    first = 0
    for width, (top, bot) in zip(PARTS, ends):
        sent = azimuth(first, width, own, top, bot, edges, tables)
        cells.append(lax.all_to_all(sent, "range", split_axis=0, concat_axis=0, tiled=True))
        first += width
    return tuple(range_transform(PARTS, cells, range_tables(PARTS)))


def solution(mesh):
    placed = (
        P("pulse", "range"),
        P("pulse", "range"),
        P("pulse", None, None, None),
        P("pulse", None),
        P("pulse"),
    )
    return jax.shard_map(
        shards,
        mesh=mesh,
        in_specs=placed,
        out_specs=(P(("pulse", "range"), None), P(("pulse", "range"), None)),
        check_vma=False,
    )
```
